512 devices in a mesh: seq: 128 (over x, y, z_lo, core), batch: 4 (over z_hi).
Axes of the slice: x: 4, y: 8, z: 8 (z_hi: 4, z_lo: 2; z = z_hi * 2 + z_lo), core: 2. Of those that a mesh axis runs over, the one named last changes fastest.
Arguments:
- queries: bfloat16 [65536, 1024], P(('batch', 'seq')), parts along dimension 0, may hold values from -150 to 150
- key_rows: bfloat16 [65536, 1024], P(('batch', 'seq')), parts along dimension 0, may hold values from -6 to 6
- value_rows: bfloat16 [65536, 1024], P(('batch', 'seq')), parts along dimension 0, may hold values from -6 to 6
- cotangent: bfloat16 [65536, 1024], P(('batch', 'seq')), parts along dimension 0, may hold values from -6 to 6
- matches: int32 [12, 128], P('batch'), parts along dimension 0, may hold values from 0 to 127, as said below
- active: int32 [12, 128], P('batch', 'seq'), parts along dimension 0, may hold values from 0 to 1, as said below
- global_pos: int32 [2048], P(('batch', 'seq')), parts along dimension 0, may hold values from 0 to 16383, as said below
Outputs:
- attended: bfloat16 [65536, 1024], P(('batch', 'seq')), parts along dimension 0
- query_grad: bfloat16 [65536, 1024], P(('batch', 'seq')), parts along dimension 0
- key_grad: bfloat16 [65536, 1024], P(('batch', 'seq')), parts along dimension 0
- value_grad: bfloat16 [65536, 1024], P(('batch', 'seq')), parts along dimension 0
The draws below stay inside these ranges and needn't reach their ends.
There are 4 independent parts, one for each index of `batch`. The reference program is written for one: setup_inputs(seed, part) draws one part's arguments, and reference() takes and returns one part's arrays. A program takes and returns all parts, laid end to end along the dimension named above; each array names one. Nothing has to cross between parts.
Inputs may be any that keep to these rules, and one draw needn't show every extreme that they name: Each row r pairs the shards: matches[r, matches[r, s]] = s and matches[r, s] != s. Symmetric within each pair: active[r, s] = active[r, matches[r, s]]. `global_pos`: entries s * 4 to (s + 1) * 4 - 1 are increasing positions inside shard s.
All inputs are finite; a program needn't handle non-finite values.
Results may differ from the reference program's by a relative error of at most 0.018.
Values may be sent and summed in bfloat16 or wider, within the bound.
A program may use at most 64 MiB of HBM per device.

```python
import jax
import jax.numpy as jnp
from jax import lax

HEAD_DIM = 128
WIDTH = 1024
TOK_DEV = 128
ROUNDS = 3
GLOB_DEV = 4
TOKENS = 16384
GLOBALS = 512
N_SEQ = 128


def pair_orders(key):
    return [jax.random.permutation(jax.random.fold_in(key, 100 + match_no), N_SEQ).astype(jnp.int32) for match_no in range(ROUNDS)]


def key_base(key):
    return jnp.clip(jax.random.normal(key, (TOKENS, WIDTH), jnp.float32), -6.0, 6.0)


def draw_matches(key, part):
    shuffles = pair_orders(key)
    rows_out = []
    for shuffled in shuffles:
        partners = shuffled.reshape(-1, 2)[:, ::-1].reshape(-1)
        rows_out.append(jnp.zeros((N_SEQ,), jnp.int32).at[shuffled].set(partners))
    return jnp.stack(rows_out)


def draw_active(key, part):
    own_key = jax.random.fold_in(key, 2)
    shuffles = pair_orders(key)
    flags = (jax.random.randint(own_key, (ROUNDS, N_SEQ // 2), 0, 4) > 0).astype(jnp.int32)
    flags = flags.at[0, 0].set(0).at[0, 1].set(1)
    rows_out = []
    for match_no in range(ROUNDS):
        rows_out.append(jnp.zeros((N_SEQ,), jnp.int32).at[shuffles[match_no]].set(jnp.repeat(flags[match_no], 2)))
    return jnp.stack(rows_out)


def draw_global_pos(key, part):
    own_key = jax.random.fold_in(key, 3)
    stride_len = TOK_DEV // GLOB_DEV
    jitter = jax.random.randint(own_key, (N_SEQ, GLOB_DEV), 0, stride_len)
    jitter = jitter.at[0, 0].set(0).at[N_SEQ - 1, GLOB_DEV - 1].set(stride_len - 1)
    starts = jnp.arange(N_SEQ, dtype=jnp.int32)[:, None] * TOK_DEV + jnp.arange(GLOB_DEV, dtype=jnp.int32)[None, :] * stride_len
    return (starts + jitter).astype(jnp.int32).reshape(-1)


def draw_key_rows(key, part):
    base = key_base(key)
    return base.astype(jnp.bfloat16)


def draw_queries(key, part):
    own_key = jax.random.fold_in(key, 5)
    fresh = jnp.clip(jax.random.normal(own_key, (TOKENS, WIDTH), jnp.float32), -6.0, 6.0) * 2.5
    return fresh.astype(jnp.bfloat16)


def block_levels(rng, dims, shards, least, top_value):
    loudness, own = 1.0, jax.random.fold_in(rng, 6)
    for position, blocks in shards:
        steps = jnp.exp(jax.random.uniform(jax.random.fold_in(own, position), (blocks,), jnp.float32, least / len(shards), top_value / len(shards)))
        loudness = loudness * jnp.repeat(steps, dims[position] // blocks).reshape([-1 if axis == position else 1 for axis in range(len(dims))])
    return loudness


def noise(key, extent, width, bound, pieces=(), kind=jnp.bfloat16):
    result = jax.random.normal(key, extent, jnp.float32) * width
    if len(pieces) > 0:
        result = block_levels(key, extent, pieces, -0.22, 0.18) * result
    return jnp.clip(result, min=-bound, max=bound).astype(kind)


def setup_inputs(seed: int = 0, part: int = 0) -> dict:
    keys = jax.random.split(jax.random.key(seed), 8)
    part_keys = jax.random.split(jax.random.fold_in(keys[7], part), 8)
    queries = draw_queries(jax.random.fold_in(jax.random.fold_in(keys[7], part), 71), part)
    key_rows = draw_key_rows(jax.random.fold_in(jax.random.fold_in(keys[7], part), 71), part)
    value_rows = noise(part_keys[2], (TOKENS, WIDTH), 1.0, 6.0, ((0, 128),))
    cotangent = noise(part_keys[3], (TOKENS, WIDTH), 1.0, 6.0, ((0, 128),))
    matches = draw_matches(jax.random.fold_in(jax.random.fold_in(keys[7], part), 71), part)
    active = draw_active(jax.random.fold_in(jax.random.fold_in(keys[7], part), 71), part)
    global_pos = draw_global_pos(jax.random.fold_in(jax.random.fold_in(keys[7], part), 71), part)
    return dict(queries=queries, key_rows=key_rows, value_rows=value_rows, cotangent=cotangent, matches=matches, active=active, global_pos=global_pos)


masked_score = -1.0e30


def reference(queries, key_rows, value_rows, cotangent, matches, active, global_pos):
    tokens, feat_width = queries.shape
    head_count = feat_width // HEAD_DIM
    scaling = HEAD_DIM ** -0.5
    local_count = (ROUNDS + 1) * TOK_DEV
    query_blocks = queries.reshape(N_SEQ, TOK_DEV, head_count, HEAD_DIM)
    key_blocks = key_rows.reshape(N_SEQ, TOK_DEV, head_count, HEAD_DIM)
    value_blocks = value_rows.reshape(N_SEQ, TOK_DEV, head_count, HEAD_DIM)
    grad_blocks = cotangent.reshape(N_SEQ, TOK_DEV, head_count, HEAD_DIM)
    global_keys = jnp.take(key_rows, global_pos, axis=0).reshape(GLOBALS, head_count, HEAD_DIM)
    global_values = jnp.take(value_rows, global_pos, axis=0).reshape(GLOBALS, head_count, HEAD_DIM)

    def one_shard(carry, shard):
        partner_ids = [matches[match_no, shard] for match_no in range(ROUNDS)]
        all_keys = jnp.concatenate([key_blocks[shard]] + [key_blocks[pid] for pid in partner_ids] + [global_keys], axis=0).astype(jnp.float32)
        all_values = jnp.concatenate([value_blocks[shard]] + [value_blocks[pid] for pid in partner_ids] + [global_values], axis=0).astype(jnp.float32)
        query_heads = query_blocks[shard].astype(jnp.float32)
        grad_heads = grad_blocks[shard].astype(jnp.float32)
        keep = jnp.concatenate([jnp.ones((TOK_DEV,), jnp.int32), jnp.repeat(active[:, shard], TOK_DEV), jnp.ones((GLOBALS,), jnp.int32)]) > 0
        scores = jnp.einsum("qhe,khe->hqk", query_heads, all_keys) * scaling
        scores = jnp.where(keep[None, None, :], scores, masked_score)
        peak = jnp.max(scores, axis=2, keepdims=True)
        raw_weights = jnp.exp(scores - peak)
        probs = raw_weights / jnp.sum(raw_weights, axis=2, keepdims=True)
        probs_low = lax.optimization_barrier(probs.astype(jnp.bfloat16)).astype(jnp.float32)
        mixed = jnp.einsum("hqk,khe->qhe", probs_low, all_values)
        grad_probs = jnp.einsum("qhe,khe->hqk", grad_heads, all_values)
        centre = jnp.sum(grad_heads * mixed, axis=2)
        score_grad = (probs * (grad_probs - centre.T[:, :, None])).astype(jnp.bfloat16)
        score_grad = lax.optimization_barrier(score_grad).astype(jnp.float32)
        query_grad = (jnp.einsum("hqk,khe->qhe", score_grad, all_keys) * scaling).astype(jnp.bfloat16)
        grad_split = score_grad[:, :, :local_count].reshape(head_count, TOK_DEV, ROUNDS + 1, TOK_DEV)
        prob_split = probs_low[:, :, :local_count].reshape(head_count, TOK_DEV, ROUNDS + 1, TOK_DEV)
        key_terms = (jnp.einsum("hqrt,qhe->trhe", grad_split, query_heads) * scaling).reshape(TOK_DEV, ROUNDS + 1, feat_width)
        value_terms = jnp.einsum("hqrt,qhe->trhe", prob_split, grad_heads).reshape(TOK_DEV, ROUNDS + 1, feat_width)
        glob_key = jnp.einsum("hqk,qhe->khe", score_grad[:, :, local_count:], query_heads) * scaling
        glob_value = jnp.einsum("hqk,qhe->khe", probs_low[:, :, local_count:], grad_heads)
        carry = carry + jnp.concatenate([glob_key.reshape(GLOBALS, feat_width), glob_value.reshape(GLOBALS, feat_width)], axis=1)
        outputs = (mixed.astype(jnp.bfloat16).reshape(TOK_DEV, feat_width), query_grad.reshape(TOK_DEV, feat_width),
                   key_terms[:, 0], key_terms[:, 1:].astype(jnp.bfloat16), value_terms[:, 0], value_terms[:, 1:].astype(jnp.bfloat16))
        return carry, outputs

    start_sum = jnp.zeros((GLOBALS, 2 * feat_width), jnp.float32)
    glob_sum, outputs = lax.scan(one_shard, start_sum, jnp.arange(N_SEQ, dtype=jnp.int32))
    attended_blocks, query_grad_blocks, own_keys, sent_keys, own_values, sent_values = outputs
    key_total = own_keys
    value_total = own_values
    for match_no in range(ROUNDS):
        key_total = key_total + jnp.take(sent_keys[:, :, match_no], matches[match_no], axis=0).astype(jnp.float32)
        value_total = value_total + jnp.take(sent_values[:, :, match_no], matches[match_no], axis=0).astype(jnp.float32)
    key_total = key_total.reshape(tokens, feat_width).at[global_pos].add(glob_sum[:, :feat_width])
    value_total = value_total.reshape(tokens, feat_width).at[global_pos].add(glob_sum[:, feat_width:])
    attended = attended_blocks.reshape(tokens, feat_width)
    query_grad = query_grad_blocks.reshape(tokens, feat_width)
    return attended, query_grad, key_total.astype(jnp.bfloat16), value_total.astype(jnp.bfloat16)
```

```python
import jax
import jax.numpy as jnp
from jax import lax
from jax.experimental import pallas as pl
from jax.experimental.pallas import tpu as pltpu
from jax.sharding import PartitionSpec as P

HD = 128
ROUNDS = 3
NY = 8
NP = 16
TOK = 128
SCALE = HD**-0.5
LOG2E = 1.4426950408889634
BF = jnp.bfloat16
F32 = jnp.float32


def mm(a, b):
    return lax.dot_general(a, b, (((1,), (0,)), ((), ())), preferred_element_type=F32)


def mm_t(a, b):
    return lax.dot_general(a, b, (((1,), (1,)), ((), ())), preferred_element_type=F32)


def kernel(
    matches, active, gpos, q_in, k_in, v_in, g_in,
    o_out, dq_out, dk_out, dv_out,
    aux, aux_all, kv, qg, inter, stage, part, gl_mine, gl_all,
    k_all, v_all, ret_stage, ret, tot_stage, tot, own, gacc, gg_stage, gg,
    od_stage, kvg_stage,
    sem_aux, sem_kv, sem_qg, sem_inter, sem_part, sem_gl, sem_ret, sem_tot, sem_gg, sem_out,
    send_aux, send_kv, send_qg, send_inter, send_part, send_gl, send_ret, send_tot, send_gg, send_od, send_kvg,
):
    me = lax.axis_index("seq")
    my_x, my_y, my_zc = me // 32, (me // 4) % NY, me % 4
    my_p = my_x * 4 + my_zc

    def line(y):
        return {"seq": my_x * 32 + y * 4 + my_zc}

    def plane(p):
        return {"seq": (p // 4) * 32 + my_y * 4 + p % 4}

    def put(src, dst, send, recv, where):
        pltpu.make_async_remote_copy(
            src_ref=src, dst_ref=dst, send_sem=send, recv_sem=recv, device_id=where,
            device_id_type=pl.DeviceIdType.MESH,
        ).start()

    def keep(src, dst, recv):
        pltpu.make_async_copy(src, dst, recv).start()

    def wait(ref, sem):
        pltpu.make_async_copy(ref, ref, sem).wait()

    def cols(ref, y):
        return ref.at[:, pl.ds(pl.multiple_of(y * HD, HD), HD)]

    barrier = pltpu.get_barrier_semaphore()

    @pl.loop(1, NY)
    def _(n):
        pl.semaphore_signal(barrier, inc=1, device_id=line((my_y + n) % NY), device_id_type=pl.DeviceIdType.MESH)

    @pl.loop(1, NP)
    def _(n):
        pl.semaphore_signal(barrier, inc=1, device_id=plane((my_p + n) % NP), device_id_type=pl.DeviceIdType.MESH)

    row = lax.broadcasted_iota(jnp.int32, (32, TOK), 0)
    lane = lax.broadcasted_iota(jnp.int32, (32, TOK), 1)
    tile = jnp.zeros((32, TOK), F32)
    for n in range(4):
        here = (row == (my_y % 4) * 4 + n) & (lane == gpos[n] - me * TOK)
        tile = jnp.where(here, 1.0, tile)
    for r in range(ROUNDS):
        tile = jnp.where(row == 16 + r, active[r, 0].astype(F32), tile)
    aux[...] = tile.astype(BF)

    pl.semaphore_wait(barrier, NY - 1 + NP - 1)

    keep(aux, aux_all.at[my_y], sem_aux)
    keep(cols(k_in, my_y), kv.at[0, my_y], sem_kv)
    keep(cols(v_in, my_y), kv.at[1, my_y], sem_kv)
    keep(cols(q_in, my_y), qg.at[0, my_y], sem_qg)
    keep(cols(g_in, my_y), qg.at[1, my_y], sem_qg)

    @pl.loop(1, NY)
    def _(n):
        y = (my_y + n) % NY
        put(aux, aux_all.at[my_y], send_aux, sem_aux, line(y))
        put(cols(k_in, y), kv.at[0, my_y], send_kv, sem_kv, line(y))
        put(cols(v_in, y), kv.at[1, my_y], send_kv, sem_kv, line(y))

    @pl.loop(1, NY)
    def _(n):
        y = (my_y + n) % NY
        put(cols(q_in, y), qg.at[0, my_y], send_qg, sem_qg, line(y))
        put(cols(g_in, y), qg.at[1, my_y], send_qg, sem_qg, line(y))

    wait(kv, sem_kv)

    def tile_of(p):
        return kv.at[p % 2, :, pl.ds(pl.multiple_of((p // 2) * 16, 16), 16), :]

    keep(tile_of(my_p), inter.at[my_x, :, my_zc], sem_inter)

    @pl.loop(1, NP)
    def _(n):
        p = (my_p + n) % NP
        put(tile_of(p), inter.at[my_x, :, my_zc], send_inter, sem_inter, plane(p))

    wait(aux_all, sem_aux)
    for half in range(2):
        picks = jnp.concatenate([aux_all[half * 4 + n, :16] for n in range(4)], axis=1)
        for which in range(2):
            rows = kv[which, half * 4 : half * 4 + 4].reshape(4 * TOK, HD)
            gl_mine[which, half * 16 : half * 16 + 16] = mm(picks, rows).astype(BF)
    keep(gl_mine, gl_all.at[my_p], sem_gl)

    @pl.loop(1, NP)
    def _(n):
        put(gl_mine, gl_all.at[my_p], send_gl, sem_gl, plane((my_p + n) % NP))

    wait(inter, sem_inter)

    def pick(p):
        for t in range(NY):
            s = (p // 4) * 32 + t * 4 + p % 4
            for r in range(ROUNDS):
                m = matches[r, s]
                stage[p, t, r] = inter[m // 32, (m // 4) % NY, m % 4]

    @pl.loop(1, NP)
    def _(n):
        p = (my_p + n) % NP
        pick(p)
        put(stage.at[p], part.at[my_p // 2, my_p % 2], send_part, sem_part, plane(p))

    pick(my_p)
    keep(stage.at[my_p], part.at[my_p // 2, my_p % 2], sem_part)

    wait(gl_all, sem_gl)
    k_all[512:] = gl_all[:, 0].reshape(512, HD)
    v_all[512:] = gl_all[:, 1].reshape(512, HD)
    gacc[...] = jnp.zeros_like(gacc)
    wait(qg, sem_qg)
    wait(part, sem_part)

    @pl.loop(0, NY)
    def _(n):
        t = (my_y + n) % NY
        q, g = qg[0, t], qg[1, t]
        k_all[0:TOK] = kv[0, t]
        v_all[0:TOK] = kv[1, t]
        for r in range(ROUNDS):
            k_all[TOK * (r + 1) : TOK * (r + 2)] = part[:, 0, t, r].reshape(TOK, HD)
            v_all[TOK * (r + 1) : TOK * (r + 2)] = part[:, 1, t, r].reshape(TOK, HD)
        keys, values = k_all[...], v_all[...]
        flags = [aux_all[t, 16:32].astype(F32)[r : r + 1] for r in range(ROUNDS)]
        bias = jnp.concatenate(
            [jnp.zeros((1, TOK), F32)] + [(f - 1.0) * 1e30 for f in flags] + [jnp.zeros((1, 512), F32)], axis=1
        )
        scores = mm_t(q, keys) * (SCALE * LOG2E) + bias
        weights = jnp.exp2(scores - jnp.max(scores, axis=1, keepdims=True))
        probs = weights * (1.0 / jnp.sum(weights, axis=1, keepdims=True))
        low = probs.astype(BF)
        gp = mm_t(g, values)
        centre = jnp.sum(low.astype(F32) * gp, axis=1, keepdims=True)
        sg = (probs * (gp - centre)).astype(BF)
        od_stage[0, t] = mm(low, values).astype(BF)
        od_stage[1, t] = (mm(sg, keys) * SCALE).astype(BF)

        @pl.when(n == 0)
        def _():
            keep(od_stage.at[0, t], cols(o_out, my_y), sem_out.at[0])
            keep(od_stage.at[1, t], cols(dq_out, my_y), sem_out.at[1])

        @pl.when(n > 0)
        def _():
            put(od_stage.at[0, t], cols(o_out, my_y), send_od, sem_out.at[0], line(t))
            put(od_stage.at[1, t], cols(dq_out, my_y), send_od, sem_out.at[1], line(t))

        kt = mm(q.T, sg) * SCALE
        vt = mm(g.T, low)
        for which, term in ((0, kt), (1, vt)):
            own[which, t] = term[:, :TOK]
            for r in range(ROUNDS):
                ret_stage[:, which, t, r] = term[:, TOK * (r + 1) : TOK * (r + 2)].astype(BF).reshape(8, 16, TOK)
            gacc[which] += term[:, 512:]

        keep(ret_stage.at[my_p // 2, my_p % 2, t], ret.at[my_x, t, my_zc], sem_ret)

        @pl.loop(1, NP)
        def _(i):
            p = (my_p + i) % NP
            put(ret_stage.at[p // 2, p % 2, t], ret.at[my_x, t, my_zc], send_ret, sem_ret, plane(p))

    for which in range(2):
        gg_stage[:, which] = gacc[which].T.astype(BF).reshape(NP, 32, HD)
    keep(gg_stage.at[my_p], gg.at[my_p], sem_gg)

    @pl.loop(1, NP)
    def _(n):
        p = (my_p + n) % NP
        put(gg_stage.at[p], gg.at[my_p], send_gg, sem_gg, plane(p))

    wait(ret, sem_ret)

    def total(p):
        for t in range(NY):
            s = (p // 4) * 32 + t * 4 + p % 4
            terms = []
            for r in range(ROUNDS):
                m = matches[r, s]
                terms.append(ret[m // 32, (m // 4) % NY, m % 4, r].astype(F32))
            tot_stage[p, t] = (terms[0] + terms[1] + terms[2]).astype(BF)

    @pl.loop(1, NP)
    def _(n):
        p = (my_p + n) % NP
        total(p)
        put(tot_stage.at[p], tot.at[my_p // 2, my_p % 2], send_tot, sem_tot, plane(p))

    total(my_p)
    keep(tot_stage.at[my_p], tot.at[my_p // 2, my_p % 2], sem_tot)

    wait(gg, sem_gg)
    gsum = [jnp.sum(gg[:, which].astype(F32), axis=0) for which in range(2)]
    for which in range(2):
        gacc[which, :32, :HD] = gsum[which]
    wait(tot, sem_tot)

    @pl.loop(0, NY)
    def _(n):
        t = (my_y + n) % NY
        spots = aux_all[t, :16]
        for which, out in ((0, dk_out), (1, dv_out)):
            rows = gacc[which, pl.ds(pl.multiple_of((t // 4) * 16, 16), 16), :HD].astype(BF)
            back = own[which, t] + tot[:, which, t].reshape(HD, TOK).astype(F32)
            there = lax.dot_general(spots, rows, (((0,), (0,)), ((), ())), preferred_element_type=F32)
            kvg_stage[which, t] = (back.T + there).astype(BF)

            @pl.when(n == 0)
            def _():
                keep(kvg_stage.at[which, t], cols(out, my_y), sem_out.at[2 + which])

            @pl.when(n > 0)
            def _():
                put(kvg_stage.at[which, t], cols(out, my_y), send_kvg, sem_out.at[2 + which], line(t))

    wait(o_out, sem_out.at[0])
    wait(dq_out, sem_out.at[1])
    wait(dk_out, sem_out.at[2])
    wait(dv_out, sem_out.at[3])
    wait(aux_all.at[: NY - 1], send_aux)
    for sem in (send_kv, send_qg, send_od, send_kvg):
        wait(kv.at[:, : NY - 1], sem)
    for sem in (send_inter, send_tot):
        wait(tot_stage.at[: NP - 1], sem)
    for sem in (send_part, send_ret):
        wait(stage.at[: NP - 1], sem)
    for sem in (send_gl, send_gg):
        wait(gg_stage.at[: NP - 1], sem)


def local(queries, key_rows, value_rows, cotangent, matches, active, global_pos):
    out = jax.ShapeDtypeStruct(queries.shape, BF)
    smem, vmem, hbm = (pl.BlockSpec(memory_space=m) for m in (pltpu.SMEM, pltpu.VMEM, pl.ANY))
    dma = pltpu.SemaphoreType.DMA
    return pl.pallas_call(
        kernel,
        out_shape=(out,) * 4,
        in_specs=[smem] * 3 + [hbm] * 4,
        out_specs=(vmem,) * 4,
        scratch_shapes=[
            pltpu.VMEM((32, TOK), BF),
            pltpu.VMEM((NY, 32, TOK), BF),
            pltpu.VMEM((2, NY, TOK, HD), BF),
            pltpu.VMEM((2, NY, TOK, HD), BF),
            pltpu.VMEM((4, NY, 4, 16, HD), BF),
            pltpu.VMEM((NP, NY, ROUNDS, 16, HD), BF),
            pltpu.VMEM((8, 2, NY, ROUNDS, 16, HD), BF),
            pltpu.VMEM((2, 32, HD), BF),
            pltpu.VMEM((NP, 2, 32, HD), BF),
            pltpu.VMEM((1024, HD), BF),
            pltpu.VMEM((1024, HD), BF),
            pltpu.VMEM((8, 2, NY, ROUNDS, 16, TOK), BF),
            pltpu.VMEM((4, NY, 4, ROUNDS, 16, TOK), BF),
            pltpu.VMEM((NP, NY, 16, TOK), BF),
            pltpu.VMEM((8, 2, NY, 16, TOK), BF),
            pltpu.VMEM((2, NY, HD, TOK), F32),
            pltpu.VMEM((2, HD, 512), F32),
            pltpu.VMEM((NP, 2, 32, HD), BF),
            pltpu.VMEM((NP, 2, 32, HD), BF),
            pltpu.VMEM((2, NY, TOK, HD), BF),
            pltpu.VMEM((2, NY, TOK, HD), BF),
        ]
        + [dma] * 9
        + [dma((4,))]
        + [dma] * 11,
        compiler_params=pltpu.CompilerParams(
            collective_id=0, has_side_effects=True, vmem_limit_bytes=48 * 1024 * 1024
        ),
        cost_estimate=pl.CostEstimate(flops=1_700_000_000, bytes_accessed=2_000_000, transcendentals=1_048_576),
    )(matches, active, global_pos, queries, key_rows, value_rows, cotangent)


def solution(mesh):
    rows = P(("batch", "seq"), None)
    return jax.shard_map(
        local,
        mesh=mesh,
        in_specs=(rows, rows, rows, rows, P("batch", None), P("batch", "seq"), P(("batch", "seq"))),
        out_specs=(rows,) * 4,
        check_vma=False,
    )
```

```python
import jax
import jax.numpy as jnp
from jax import lax
from jax.experimental import pallas as pl
from jax.experimental.pallas import tpu as pltpu
from jax.sharding import PartitionSpec as P

HD = 128
ROUNDS = 3
NY = 8
NP = 16
TOK = 128
SCALE = HD**-0.5
LOG2E = 1.4426950408889634
BF = jnp.bfloat16
F32 = jnp.float32


def mm(a, b):
    return lax.dot_general(a, b, (((1,), (0,)), ((), ())), preferred_element_type=F32)


def mm_t(a, b):
    return lax.dot_general(a, b, (((1,), (1,)), ((), ())), preferred_element_type=F32)


def kernel(
    matches, active, gpos, q_in, k_in, v_in, g_in,
    o_out, dq_out, dk_out, dv_out,
    aux, aux_all, kv, qg, inter, stage, part, gl_mine, gl_all,
    k_loc, k_glob, v_loc, v_glob, probs, low, sgrad, q_t, g_t,
    ret_stage, ret, tot_stage, tot, own, gg_stage, gg, gsum, od_stage, kvg_stage,
    sem_aux, sem_kv, sem_qg, sem_inter, sem_part, sem_gl, sem_ret, sem_tot, sem_gg, sem_out,
    send_aux, send_kv, send_qg, send_inter, send_part, send_gl, send_ret, send_tot, send_gg, send_od, send_kvg,
):
    me = lax.axis_index("seq")
    my_x, my_y, my_zc = me // 32, (me // 4) % NY, me % 4
    my_z, my_core = my_zc // 2, my_zc % 2
    my_p = my_x * 4 + my_zc

    def shard(p, y):
        return (p // 4) * 32 + y * 4 + p % 4

    def line(y):
        return {"seq": shard(my_p, y)}

    def plane(p):
        return {"seq": shard(p, my_y)}

    def line_step(n):
        return (n + 1) // 2 * (1 - 2 * ((n + 1) % 2))

    def line_to(n):
        return (my_y + NY + line_step(n)) % NY

    def line_from(n):
        return (my_y + NY - line_step(n)) % NY

    def plane_to(n):
        return (my_x + n) % 4 * 4 + (my_zc + n + n // 4) % 4

    def chip_to(n):
        return (my_x + n) % 4 * 2 + (my_z + n + n // 4) % 2

    def put(src, dst, send, recv, where):
        pltpu.make_async_remote_copy(
            src_ref=src, dst_ref=dst, send_sem=send, recv_sem=recv, device_id=where,
            device_id_type=pl.DeviceIdType.MESH,
        ).start()

    def keep(src, dst, recv):
        pltpu.make_async_copy(src, dst, recv).start()

    def wait(ref, sem):
        pltpu.make_async_copy(ref, ref, sem).wait()

    def cols(ref, y):
        return ref.at[:, pl.ds(pl.multiple_of(y * HD, HD), HD)]

    def to_keepers(which, src, dst, send, recv):
        @pl.loop(0, 8)
        def _(i):
            tile = chip_to(i)
            here = jnp.logical_and(i == 0, my_core == which)

            @pl.when(here)
            def _():
                keep(src(tile), dst, recv)

            @pl.when(jnp.logical_not(here))
            def _():
                put(src(tile), dst, send, recv, plane(tile * 2 + which))

    barrier = pltpu.get_barrier_semaphore()

    @pl.loop(1, NY)
    def _(n):
        pl.semaphore_signal(barrier, inc=1, device_id=line(line_to(n)), device_id_type=pl.DeviceIdType.MESH)

    @pl.loop(1, NP)
    def _(n):
        pl.semaphore_signal(barrier, inc=1, device_id=plane(plane_to(n)), device_id_type=pl.DeviceIdType.MESH)

    row = lax.broadcasted_iota(jnp.int32, (32, TOK), 0)
    lane = lax.broadcasted_iota(jnp.int32, (32, TOK), 1)
    tile = jnp.zeros((32, TOK), F32)
    for n in range(4):
        here = (row == (my_y % 4) * 4 + n) & (lane == gpos[n] - me * TOK)
        tile = jnp.where(here, 1.0, tile)
    for r in range(ROUNDS):
        tile = jnp.where(row == 16 + r, active[r].astype(F32), tile)
    aux[...] = tile.astype(BF)

    pl.semaphore_wait(barrier, NY - 1 + NP - 1)

    @pl.loop(1, NY)
    def _(n):
        put(cols(k_in, line_to(n)), kv.at[0, my_y], send_kv, sem_kv.at[0, my_y], line(line_to(n)))

    keep(cols(k_in, my_y), kv.at[0, my_y], sem_kv.at[0, my_y])
    keep(cols(v_in, my_y), kv.at[1, my_y], sem_kv.at[1, my_y])
    keep(cols(q_in, my_y), qg.at[0, my_y], sem_qg.at[0])
    keep(cols(g_in, my_y), qg.at[1, my_y], sem_qg.at[1])
    keep(aux, aux_all.at[my_y], sem_aux)

    @pl.loop(1, NY)
    def _(n):
        put(aux, aux_all.at[my_y], send_aux, sem_aux, line(line_to(n)))

    def hand_on(which, t):
        wait(kv.at[which, t], sem_kv.at[which, t])
        to_keepers(
            which,
            lambda tile: kv.at[which, t, pl.ds(pl.multiple_of(tile * 16, 16), 16), :],
            inter.at[shard(my_p, t)], send_inter, sem_inter,
        )

    def pick_and_send():
        wait(inter, sem_inter)

        def pick(p):
            for t in range(NY):
                for r in range(ROUNDS):
                    stage[p, t, r] = inter[matches[r, shard(p, t)]]

        dst, sem = part.at[my_p // 2, my_core], sem_part.at[my_core]

        @pl.loop(1, NP)
        def _(n):
            p = plane_to(n)
            pick(p)
            put(stage.at[p], dst, send_part, sem, plane(p))

        pick(my_p)
        keep(stage.at[my_p], dst, sem)

    @pl.loop(0, NY)
    def _(n):
        hand_on(0, line_from(n))

        @pl.when(n > 0)
        def _():
            put(cols(v_in, line_to(n)), kv.at[1, my_y], send_kv, sem_kv.at[1, my_y], line(line_to(n)))

    @pl.when(my_core == 0)
    def _():
        pick_and_send()

    @pl.loop(0, NY)
    def _(n):
        hand_on(1, line_from(n))

        @pl.when(n > 0)
        def _():
            put(cols(q_in, line_to(n)), qg.at[0, my_y], send_qg, sem_qg.at[0], line(line_to(n)))

    @pl.loop(1, NY)
    def _(n):
        put(cols(g_in, line_to(n)), qg.at[1, my_y], send_qg, sem_qg.at[1], line(line_to(n)))

    wait(aux_all, sem_aux)
    for half in range(2):
        picks = jnp.concatenate([aux_all[half * 4 + n, :16] for n in range(4)], axis=1)
        for which in range(2):
            rows = kv[which, half * 4 : half * 4 + 4].reshape(4 * TOK, HD)
            gl_mine[which, half * 16 : half * 16 + 16] = mm(picks, rows).astype(BF)
    keep(gl_mine, gl_all.at[my_p], sem_gl)

    @pl.loop(1, NP)
    def _(n):
        put(gl_mine, gl_all.at[my_p], send_gl, sem_gl, plane(plane_to(n)))

    @pl.when(my_core == 1)
    def _():
        pick_and_send()

    wait(gl_all, sem_gl)
    k_glob[...] = gl_all[:, 0].reshape(512, HD)
    v_glob[...] = gl_all[:, 1].reshape(512, HD)
    wait(qg.at[0], sem_qg.at[0])
    wait(part.at[:, 0], sem_part.at[0])

    @pl.loop(0, NY)
    def _(t):
        q = qg[0, t]
        k_loc[t, 0:TOK] = kv[0, t]
        for r in range(ROUNDS):
            k_loc[t, TOK * (r + 1) : TOK * (r + 2)] = part[:, 0, t, r].reshape(TOK, HD)
        flags = aux_all[t, 16:32].astype(F32)
        bias = jnp.concatenate(
            [jnp.zeros((1, TOK), F32)] + [(flags[r : r + 1] - 1.0) * 1e30 for r in range(ROUNDS)], axis=1
        )
        s_loc = mm_t(q, k_loc[t]) * (SCALE * LOG2E) + bias
        s_glob = mm_t(q, k_glob[...]) * (SCALE * LOG2E)
        peak = jnp.maximum(jnp.max(s_loc, axis=1, keepdims=True), jnp.max(s_glob, axis=1, keepdims=True))
        w_loc, w_glob = jnp.exp2(s_loc - peak), jnp.exp2(s_glob - peak)
        inverse = 1.0 / (jnp.sum(w_loc, axis=1, keepdims=True) + jnp.sum(w_glob, axis=1, keepdims=True))
        p_loc, p_glob = w_loc * inverse, w_glob * inverse
        rows = pl.ds(pl.multiple_of(t * TOK, TOK), TOK)
        probs[rows, :512] = p_loc
        probs[rows, 512:] = p_glob
        low[rows, :512] = p_loc.astype(BF)
        low[rows, 512:] = p_glob.astype(BF)

    def give_back(which, t, term):
        own[which, t] = term[:, :TOK]
        for r in range(ROUNDS):
            ret_stage[:, which, t, r] = term[:, TOK * (r + 1) : TOK * (r + 2)].astype(BF).reshape(8, 16, TOK)
        to_keepers(
            which, lambda tile: ret_stage.at[tile, which, t], ret.at[shard(my_p, t)], send_ret, sem_ret
        )

    def give_globals(which, term):
        gg_stage[which] = term.T.astype(BF).reshape(NP, 32, HD)
        keep(gg_stage.at[which, my_p], gg.at[which, my_p], sem_gg.at[which])

        @pl.loop(1, NP)
        def _(n):
            p = plane_to(n)
            put(gg_stage.at[which, p], gg.at[which, my_p], send_gg, sem_gg.at[which], plane(p))

    wait(qg.at[1], sem_qg.at[1])

    @pl.loop(0, NY)
    def _(t):
        rows = pl.ds(pl.multiple_of(t * TOK, TOK), TOK)
        gt = qg[1, t].T
        g_t[:, rows] = gt
        give_back(1, t, mm(gt, low[rows, :512]))

    give_globals(1, mm(g_t[...], low[:, 512:]))

    wait(part.at[:, 1], sem_part.at[1])

    @pl.loop(0, NY)
    def _(n):
        t = line_to(n)
        rows = pl.ds(pl.multiple_of(t * TOK, TOK), TOK)
        q, g = qg[0, t], qg[1, t]
        v_loc[0:TOK] = kv[1, t]
        for r in range(ROUNDS):
            v_loc[TOK * (r + 1) : TOK * (r + 2)] = part[:, 1, t, r].reshape(TOK, HD)
        gp_loc, gp_glob = mm_t(g, v_loc[...]), mm_t(g, v_glob[...])
        low_loc, low_glob = low[rows, :512], low[rows, 512:]
        centre = jnp.sum(low_loc.astype(F32) * gp_loc, axis=1, keepdims=True) + jnp.sum(
            low_glob.astype(F32) * gp_glob, axis=1, keepdims=True
        )
        sg_loc = (probs[rows, :512] * (gp_loc - centre)).astype(BF)
        sg_glob = (probs[rows, 512:] * (gp_glob - centre)).astype(BF)
        sgrad[rows] = sg_glob
        qt = q.T
        q_t[:, rows] = qt
        give_back(0, t, mm(qt, sg_loc) * SCALE)
        od_stage[0, t] = (mm(low_loc, v_loc[...]) + mm(low_glob, v_glob[...])).astype(BF)
        od_stage[1, t] = ((mm(sg_loc, k_loc[t]) + mm(sg_glob, k_glob[...])) * SCALE).astype(BF)

        @pl.when(n == 0)
        def _():
            keep(od_stage.at[0, t], cols(o_out, my_y), sem_out.at[0])
            keep(od_stage.at[1, t], cols(dq_out, my_y), sem_out.at[1])

        @pl.when(n > 0)
        def _():
            put(od_stage.at[0, t], cols(o_out, my_y), send_od, sem_out.at[0], line(t))
            put(od_stage.at[1, t], cols(dq_out, my_y), send_od, sem_out.at[1], line(t))

    give_globals(0, mm(q_t[...], sgrad[...]) * SCALE)

    def add_and_send():
        wait(ret, sem_ret)

        @pl.loop(0, NY)
        def _(n):
            t = line_to(n)
            dst, sem = tot.at[my_p // 2, my_core, t], sem_tot.at[my_core, t]

            @pl.loop(0, NP)
            def _(i):
                p = plane_to(i)
                terms = [ret[matches[r, shard(p, t)], r].astype(F32) for r in range(ROUNDS)]
                tot_stage[p, t] = (terms[0] + terms[1] + terms[2]).astype(BF)

                @pl.when(i == 0)
                def _():
                    keep(tot_stage.at[p, t], dst, sem)

                @pl.when(i > 0)
                def _():
                    put(tot_stage.at[p, t], dst, send_tot, sem, plane(p))

    def finish(which, out):
        wait(gg.at[which], sem_gg.at[which])
        gsum[...] = jnp.sum(gg[which].astype(F32), axis=0).astype(BF)

        @pl.loop(0, NY)
        def _(n):
            t = line_to(n)
            wait(tot.at[:, which, t], sem_tot.at[which, t])
            rows = gsum[pl.ds(pl.multiple_of((t // 4) * 16, 16), 16)]
            back = own[which, t] + tot[:, which, t].reshape(HD, TOK).astype(F32)
            there = lax.dot_general(aux_all[t, :16], rows, (((0,), (0,)), ((), ())), preferred_element_type=F32)
            kvg_stage[which, t] = (back.T + there).astype(BF)

            @pl.when(n == 0)
            def _():
                keep(kvg_stage.at[which, t], cols(out, my_y), sem_out.at[2 + which])

            @pl.when(n > 0)
            def _():
                put(kvg_stage.at[which, t], cols(out, my_y), send_kvg, sem_out.at[2 + which], line(t))

    @pl.when(my_core == 1)
    def _():
        add_and_send()

    finish(1, dv_out)

    @pl.when(my_core == 0)
    def _():
        add_and_send()

    finish(0, dk_out)

    for n, out in enumerate((o_out, dq_out, dk_out, dv_out)):
        wait(out, sem_out.at[n])
    wait(aux_all.at[: NY - 1], send_aux)
    for sem in (send_kv, send_qg, send_od, send_kvg):
        wait(kv.at[:, : NY - 1], sem)
    for sem in (send_inter, send_tot):
        wait(tot_stage.at[: NP - 1], sem)
    for sem in (send_part, send_ret):
        wait(stage.at[: NP - 1], sem)
    wait(gl_all.at[: NP - 1], send_gl)
    wait(gl_all.at[: NP - 1], send_gg)


def hand_out(*refs):
    ins, outs, held, sems = refs[:4], refs[4:8], refs[8], refs[9]
    come = [pltpu.make_async_copy(a, held.at[n], sems.at[0, n]) for n, a in enumerate(ins)]
    go = [pltpu.make_async_copy(held.at[n], b, sems.at[1, n]) for n, b in enumerate(outs)]
    for copy in come:
        copy.start()
    for n in range(4):
        come[n].wait()
        go[n].start()
    for copy in go:
        copy.wait()


def local(queries, key_rows, value_rows, cotangent, matches, active, global_pos):
    out = jax.ShapeDtypeStruct(queries.shape, BF)
    smem, hbm = (pl.BlockSpec(memory_space=m) for m in (pltpu.SMEM, pltpu.HBM))
    dma = pltpu.SemaphoreType.DMA
    shapes = [
        ((32, TOK), BF),
        ((NY, 32, TOK), BF),
        ((2, NY, TOK, HD), BF),
        ((2, NY, TOK, HD), BF),
        ((NP * NY, 16, HD), BF),
        ((NP, NY, ROUNDS, 16, HD), BF),
        ((8, 2, NY, ROUNDS, 16, HD), BF),
        ((2, 32, HD), BF),
        ((NP, 2, 32, HD), BF),
        ((NY, 512, HD), BF),
        ((512, HD), BF),
        ((512, HD), BF),
        ((512, HD), BF),
        ((NY * TOK, 1024), F32),
        ((NY * TOK, 1024), BF),
        ((NY * TOK, 512), BF),
        ((HD, NY * TOK), BF),
        ((HD, NY * TOK), BF),
        ((8, 2, NY, ROUNDS, 16, TOK), BF),
        ((NP * NY, ROUNDS, 16, TOK), BF),
        ((NP, NY, 16, TOK), BF),
        ((8, 2, NY, 16, TOK), BF),
        ((2, NY, HD, TOK), F32),
        ((2, NP, 32, HD), BF),
        ((2, NP, 32, HD), BF),
        ((32, HD), BF),
        ((2, NY, TOK, HD), BF),
        ((2, NY, TOK, HD), BF),
    ]
    results = pl.pallas_call(
        kernel,
        out_shape=(out,) * 4,
        in_specs=[smem] * 3 + [hbm] * 4,
        out_specs=(hbm,) * 4,
        scratch_shapes=[pltpu.VMEM(*s) for s in shapes]
        + [dma, dma((2, NY)), dma((2,)), dma, dma((2,)), dma, dma, dma((2, NY)), dma((2,)), dma((4,))]
        + [dma] * 11,
        compiler_params=pltpu.CompilerParams(
            collective_id=0, has_side_effects=True, vmem_limit_bytes=63 * 1024 * 1024
        ),
        cost_estimate=pl.CostEstimate(flops=1_700_000_000, bytes_accessed=2_000_000, transcendentals=1_048_576),
    )(matches, active.reshape(ROUNDS), global_pos, queries, key_rows, value_rows, cotangent)
    return pl.pallas_call(
        hand_out,
        out_shape=(out,) * 4,
        in_specs=[hbm] * 4,
        out_specs=(hbm,) * 4,
        scratch_shapes=[pltpu.VMEM((4, TOK, NY * HD), BF), dma((2, 4))],
        compiler_params=pltpu.CompilerParams(vmem_limit_bytes=63 * 1024 * 1024),
    )(*results)


def solution(mesh):
    rows = P(("batch", "seq"), None)
    return jax.shard_map(
        local,
        mesh=mesh,
        in_specs=(rows, rows, rows, rows, P("batch", None), P("batch", "seq"), P(("batch", "seq"))),
        out_specs=(rows,) * 4,
        check_vma=False,
    )
```

```python
import jax
import jax.numpy as jnp
from jax import lax
from jax.experimental import pallas as pl
from jax.experimental.pallas import tpu as pltpu
from jax.sharding import PartitionSpec as P

HD = 128
ROUNDS = 3
NY = 8
NP = 16
EARLY = 4
TOK = 128
SCALE = HD**-0.5
LOG2E = 1.4426950408889634
BF = jnp.bfloat16
F32 = jnp.float32


def mm(a, b):
    return lax.dot_general(a, b, (((1,), (0,)), ((), ())), preferred_element_type=F32)


def mm_t(a, b):
    return lax.dot_general(a, b, (((1,), (1,)), ((), ())), preferred_element_type=F32)


def kernel(
    matches, active, gpos, q_in, k_in, v_in, g_in,
    o_out, dq_out, dk_out, dv_out,
    moved, aux, aux_all, kv, qg, inter, stage, part, gl_mine, gl_all,
    k_loc, k_glob, v_loc, v_glob, probs, low, sgrad, q_t, g_t,
    ret_stage, ret, tot_stage, tot, own, gg_stage, gg_half, gg_pair, gg_sum, gg, gsum, od_stage, kvg_stage,
    sem_moved, sem_aux, sem_kv, sem_qg, sem_inter, sem_part, sem_gl, sem_ret, sem_tot, sem_gg, sem_out,
    send_aux, send_kv, send_qg, send_inter, send_part, send_gl, send_ret, send_tot, send_gg, send_od, send_kvg,
):
    me = lax.axis_index("seq")
    my_x, my_y, my_zc = me // 32, (me // 4) % NY, me % 4
    my_z, my_core = my_zc // 2, my_zc % 2
    my_p = my_x * 4 + my_zc
    my_chip = my_p // 2

    def shard(p, y):
        return (p // 4) * 32 + y * 4 + p % 4

    def line(y):
        return {"seq": shard(my_p, y)}

    def plane(p):
        return {"seq": shard(p, my_y)}

    def line_step(n):
        return (n + 1) // 2 * (1 - 2 * ((n + 1) % 2))

    def line_to(n):
        return (my_y + NY + line_step(n)) % NY

    def line_from(n):
        return (my_y + NY - line_step(n)) % NY

    def plane_to(n):
        return (my_x + n) % 4 * 4 + (my_zc + n + n // 4) % 4

    def turn(n):
        return line_to((n + 1) % NY)

    def far(n):
        return line_to(NY - 1 - n)

    def chip_to(n):
        return (my_x + n) % 4 * 2 + (my_z + n + n // 4) % 2

    def put(src, dst, send, recv, where):
        pltpu.make_async_remote_copy(
            src_ref=src, dst_ref=dst, send_sem=send, recv_sem=recv, device_id=where,
            device_id_type=pl.DeviceIdType.MESH,
        ).start()

    def keep(src, dst, recv):
        pltpu.make_async_copy(src, dst, recv).start()

    def wait(ref, sem):
        pltpu.make_async_copy(ref, ref, sem).wait()

    def cols(ref, y):
        return ref.at[:, pl.ds(pl.multiple_of(y * HD, HD), HD)]

    def to_keepers(which, src, dst, send, recv):
        @pl.loop(0, 8)
        def _(i):
            tile = chip_to(i)
            here = jnp.logical_and(i == 0, my_core == which)

            @pl.when(here)
            def _():
                keep(src(tile), dst, recv)

            @pl.when(jnp.logical_not(here))
            def _():
                put(src(tile), dst, send, recv, plane(tile * 2 + which))

    barrier = pltpu.get_barrier_semaphore()

    @pl.loop(1, NY)
    def _(n):
        pl.semaphore_signal(barrier, inc=1, device_id=line(line_to(n)), device_id_type=pl.DeviceIdType.MESH)

    @pl.loop(1, NP)
    def _(n):
        pl.semaphore_signal(barrier, inc=1, device_id=plane(plane_to(n)), device_id_type=pl.DeviceIdType.MESH)

    for n, ref in enumerate((k_in, v_in, q_in, g_in)):

        @pl.loop(0, NY)
        def _(y):
            keep(cols(ref, y), moved.at[n, y], sem_moved.at[n])

    row = lax.broadcasted_iota(jnp.int32, (32, TOK), 0)
    lane = lax.broadcasted_iota(jnp.int32, (32, TOK), 1)
    tile = jnp.zeros((32, TOK), F32)
    for n in range(4):
        here = (row == (my_y % 4) * 4 + n) & (lane == gpos[n] - me * TOK)
        tile = jnp.where(here, 1.0, tile)
    for r in range(ROUNDS):
        tile = jnp.where(row == 16 + r, active[r].astype(F32), tile)
    aux[...] = tile.astype(BF)
    for n in range(4):
        wait(moved.at[n], sem_moved.at[n])

    pl.semaphore_wait(barrier, NY - 1 + NP - 1)

    @pl.loop(1, NY)
    def _(n):
        put(moved.at[0, line_to(n)], kv.at[0, my_y], send_kv, sem_kv.at[0, my_y], line(line_to(n)))

    keep(moved.at[0, my_y], kv.at[0, my_y], sem_kv.at[0, my_y])
    keep(moved.at[1, my_y], kv.at[1, my_y], sem_kv.at[1, my_y])
    keep(moved.at[2, my_y], qg.at[0, my_y], sem_qg.at[0])
    keep(moved.at[3, my_y], qg.at[1, my_y], sem_qg.at[1])
    keep(aux, aux_all.at[my_y], sem_aux)

    @pl.loop(1, NY)
    def _(n):
        put(aux, aux_all.at[my_y], send_aux, sem_aux, line(line_to(n)))

    def hand_on(which, t):
        wait(kv.at[which, t], sem_kv.at[which, t])
        to_keepers(
            which,
            lambda tile: kv.at[which, t, pl.ds(pl.multiple_of(tile * 16, 16), 16), :],
            inter.at[shard(my_p, t)], send_inter, sem_inter,
        )

    def pick_and_send():
        wait(inter, sem_inter)

        @pl.loop(0, NY)
        def _(n):
            named = [[matches[r, shard(p, turn(n))] for r in range(ROUNDS)] for p in range(NP)]
            for p in range(NP):
                for r in range(ROUNDS):
                    stage[p, n, r] = inter[named[p][r]]

            dst, sem = part.at[my_chip, my_core, n], sem_part.at[my_core, n]

            @pl.loop(1, NP)
            def _(i):
                p = plane_to(i)
                put(stage.at[p, n], dst, send_part, sem, plane(p))

            keep(stage.at[my_p, n], dst, sem)

    @pl.loop(0, NY)
    def _(n):
        hand_on(0, line_from(n))

        @pl.when(n > 0)
        def _():
            put(moved.at[1, line_to(n)], kv.at[1, my_y], send_kv, sem_kv.at[1, my_y], line(line_to(n)))

    @pl.when(my_core == 0)
    def _():
        pick_and_send()

    @pl.loop(0, NY)
    def _(n):
        hand_on(1, line_from(n))

        @pl.when(n > 0)
        def _():
            put(moved.at[2, line_to(n)], qg.at[0, my_y], send_qg, sem_qg.at[0], line(line_to(n)))

    @pl.loop(1, NY)
    def _(n):
        put(moved.at[3, line_to(n)], qg.at[1, my_y], send_qg, sem_qg.at[1], line(line_to(n)))

    wait(aux_all, sem_aux)
    for half in range(2):
        picks = jnp.concatenate([aux_all[half * 4 + n, :16] for n in range(4)], axis=1)
        for which in range(2):
            rows = kv[which, half * 4 : half * 4 + 4].reshape(4 * TOK, HD)
            gl_mine[which, half * 16 : half * 16 + 16] = mm(picks, rows).astype(BF)
    keep(gl_mine, gl_all.at[my_core, my_chip], sem_gl.at[0])

    @pl.loop(1, 8)
    def _(n):
        put(gl_mine, gl_all.at[my_core, my_chip], send_gl.at[0], sem_gl.at[0], plane(chip_to(n) * 2 + my_core))

    @pl.when(my_core == 1)
    def _():
        pick_and_send()

    wait(gl_all.at[0], sem_gl.at[0])
    put(gl_all.at[my_core], gl_all.at[my_core], send_gl.at[1], sem_gl.at[1], plane(my_p + 1 - 2 * my_core))
    wait(gl_all.at[0], sem_gl.at[1])
    k_glob[...] = gl_all[:, :, 0].reshape(512, HD)
    v_glob[...] = gl_all[:, :, 1].reshape(512, HD)
    wait(qg.at[0], sem_qg.at[0])

    @pl.loop(0, NY)
    def _(n):
        t = turn(n)
        wait(part.at[:, 0, n], sem_part.at[0, n])
        q = qg[0, t]
        k_loc[t, 0:TOK] = kv[0, t]
        for r in range(ROUNDS):
            k_loc[t, TOK * (r + 1) : TOK * (r + 2)] = part[:, 0, n, r].reshape(TOK, HD)
        flags = aux_all[t, 16:32].astype(F32)
        bias = jnp.concatenate(
            [jnp.zeros((1, TOK), F32)] + [(flags[r : r + 1] - 1.0) * 1e30 for r in range(ROUNDS)], axis=1
        )
        s_loc = mm_t(q, k_loc[t]) * (SCALE * LOG2E) + bias
        s_glob = mm_t(q, k_glob[...]) * (SCALE * LOG2E)
        peak = jnp.maximum(jnp.max(s_loc, axis=1, keepdims=True), jnp.max(s_glob, axis=1, keepdims=True))
        w_loc, w_glob = jnp.exp2(s_loc - peak), jnp.exp2(s_glob - peak)
        inverse = 1.0 / (jnp.sum(w_loc, axis=1, keepdims=True) + jnp.sum(w_glob, axis=1, keepdims=True))
        p_loc, p_glob = w_loc * inverse, w_glob * inverse
        rows = pl.ds(pl.multiple_of(t * TOK, TOK), TOK)
        probs[rows, :512] = p_loc
        probs[rows, 512:] = p_glob
        low[rows, :512] = p_loc.astype(BF)
        low[rows, 512:] = p_glob.astype(BF)

    def send_back(which, t):
        to_keepers(which, lambda tile: ret_stage.at[tile, which, t], ret.at[shard(my_p, t)], send_ret, sem_ret)

    def set_terms(which, t, term):
        own[which, t] = term[:, :TOK]
        for r in range(ROUNDS):
            ret_stage[:, which, t, r] = term[:, TOK * (r + 1) : TOK * (r + 2)].astype(BF).reshape(8, 16, TOK)

    def share_globals(which, term):
        gg_stage[which] = term.T.reshape(2, 8, 32, HD)
        gg_half[which] = gg_stage[which, 1 - my_core].astype(BF)
        put(
            gg_half.at[which], gg_pair.at[which], send_gg.at[0], sem_gg.at[0, which], plane(my_p + 1 - 2 * my_core)
        )

    def give_globals(which):
        wait(gg_pair.at[which], sem_gg.at[0, which])
        gg_sum[which] = (gg_stage[which, my_core] + gg_pair[which].astype(F32)).astype(BF)
        keep(gg_sum.at[which, my_chip], gg.at[which, my_chip], sem_gg.at[1, which])

        @pl.loop(1, 8)
        def _(n):
            chip = chip_to(n)
            put(
                gg_sum.at[which, chip], gg.at[which, my_chip], send_gg.at[1], sem_gg.at[1, which],
                plane(chip * 2 + my_core),
            )

    wait(qg.at[1], sem_qg.at[1])

    @pl.loop(0, NY)
    def _(t):
        rows = pl.ds(pl.multiple_of(t * TOK, TOK), TOK)
        gt = qg[1, t].T
        g_t[:, rows] = gt
        set_terms(1, t, mm(gt, low[rows, :512]))
        send_back(1, t)

    share_globals(1, mm(g_t[...], low[:, 512:]))

    @pl.loop(0, NY)
    def _(n):
        t = turn(n)
        wait(part.at[:, 1, n], sem_part.at[1, n])
        rows = pl.ds(pl.multiple_of(t * TOK, TOK), TOK)
        q, g = qg[0, t], qg[1, t]
        v_loc[0:TOK] = kv[1, t]
        for r in range(ROUNDS):
            v_loc[TOK * (r + 1) : TOK * (r + 2)] = part[:, 1, n, r].reshape(TOK, HD)
        gp_loc, gp_glob = mm_t(g, v_loc[...]), mm_t(g, v_glob[...])
        low_loc, low_glob = low[rows, :512], low[rows, 512:]
        centre = jnp.sum(low_loc.astype(F32) * gp_loc, axis=1, keepdims=True) + jnp.sum(
            low_glob.astype(F32) * gp_glob, axis=1, keepdims=True
        )
        sg_loc = (probs[rows, :512] * (gp_loc - centre)).astype(BF)
        sg_glob = (probs[rows, 512:] * (gp_glob - centre)).astype(BF)
        sgrad[rows] = sg_glob
        qt = q.T
        q_t[:, rows] = qt
        set_terms(0, t, mm(qt, sg_loc) * SCALE)

        @pl.when(n < EARLY)
        def _():
            send_back(0, t)

        od_stage[0, t] = (mm(low_loc, v_loc[...]) + mm(low_glob, v_glob[...])).astype(BF)
        od_stage[1, t] = ((mm(sg_loc, k_loc[t]) + mm(sg_glob, k_glob[...])) * SCALE).astype(BF)

        @pl.when(n == NY - 1)
        def _():
            keep(od_stage.at[0, t], cols(o_out, my_y), sem_out.at[0])
            keep(od_stage.at[1, t], cols(dq_out, my_y), sem_out.at[1])

        @pl.when(n < NY - 1)
        def _():
            put(od_stage.at[0, t], cols(o_out, my_y), send_od, sem_out.at[0], line(t))
            put(od_stage.at[1, t], cols(dq_out, my_y), send_od, sem_out.at[1], line(t))

    def add_and_send():
        wait(ret, sem_ret)

        @pl.loop(0, NY)
        def _(n):
            t = far(n)
            dst, sem = tot.at[my_p // 2, my_core, t], sem_tot.at[my_core, t]

            named = [[matches[r, shard(p, t)] for r in range(ROUNDS)] for p in range(NP)]
            for p in range(NP):
                terms = [ret[named[p][r], r].astype(F32) for r in range(ROUNDS)]
                tot_stage[p, t] = (terms[0] + terms[1] + terms[2]).astype(BF)

            @pl.loop(1, NP)
            def _(i):
                p = plane_to(i)
                put(tot_stage.at[p, t], dst, send_tot, sem, plane(p))

            keep(tot_stage.at[my_p, t], dst, sem)

    def finish(which, out):
        wait(gg.at[which], sem_gg.at[1, which])
        gsum[...] = jnp.sum(gg[which].astype(F32), axis=0).astype(BF)

        @pl.loop(0, NY)
        def _(n):
            t = far(n)
            wait(tot.at[:, which, t], sem_tot.at[which, t])
            rows = gsum[pl.ds(pl.multiple_of((t // 4) * 16, 16), 16)]
            back = own[which, t] + tot[:, which, t].reshape(HD, TOK).astype(F32)
            there = lax.dot_general(aux_all[t, :16], rows, (((0,), (0,)), ((), ())), preferred_element_type=F32)
            kvg_stage[which, t] = (back.T + there).astype(BF)

            @pl.when(n == NY - 1)
            def _():
                keep(kvg_stage.at[which, t], cols(out, my_y), sem_out.at[2 + which])

            @pl.when(n < NY - 1)
            def _():
                put(kvg_stage.at[which, t], cols(out, my_y), send_kvg, sem_out.at[2 + which], line(t))

    give_globals(1)

    @pl.when(my_core == 1)
    def _():
        add_and_send()

    @pl.loop(EARLY, NY)
    def _(n):
        send_back(0, turn(n))

    share_globals(0, mm(q_t[...], sgrad[...]) * SCALE)
    give_globals(0)
    finish(1, dv_out)

    @pl.when(my_core == 0)
    def _():
        add_and_send()

    finish(0, dk_out)

    for n, out in enumerate((o_out, dq_out, dk_out, dv_out)):
        wait(out, sem_out.at[n])
    wait(aux_all.at[: NY - 1], send_aux)
    for sem in (send_kv, send_qg, send_od, send_kvg):
        wait(kv.at[:, : NY - 1], sem)
    for sem in (send_inter, send_tot):
        wait(tot_stage.at[: NP - 1], sem)
    for sem in (send_part, send_ret):
        wait(stage.at[: NP - 1], sem)
    wait(gl_all.at[0, :7], send_gl.at[0])
    wait(gl_all.at[0], send_gl.at[1])
    wait(gg_half, send_gg.at[0])
    wait(gg.at[:, :7], send_gg.at[1])


def hand_out(*refs):
    ins, outs, held, sems = refs[:4], refs[4:8], refs[8], refs[9]
    come = [pltpu.make_async_copy(a, held.at[n], sems.at[0, n]) for n, a in enumerate(ins)]
    go = [pltpu.make_async_copy(held.at[n], b, sems.at[1, n]) for n, b in enumerate(outs)]
    for copy in come:
        copy.start()
    for n in range(4):
        come[n].wait()
        go[n].start()
    for copy in go:
        copy.wait()


def local(queries, key_rows, value_rows, cotangent, matches, active, global_pos):
    out = jax.ShapeDtypeStruct(queries.shape, BF)
    smem, hbm = (pl.BlockSpec(memory_space=m) for m in (pltpu.SMEM, pltpu.HBM))
    dma = pltpu.SemaphoreType.DMA
    shapes = [
        ((4, NY, TOK, HD), BF),
        ((32, TOK), BF),
        ((NY, 32, TOK), BF),
        ((2, NY, TOK, HD), BF),
        ((2, NY, TOK, HD), BF),
        ((NP * NY, 16, HD), BF),
        ((NP, NY, ROUNDS, 16, HD), BF),
        ((8, 2, NY, ROUNDS, 16, HD), BF),
        ((2, 32, HD), BF),
        ((2, 8, 2, 32, HD), BF),
        ((NY, 512, HD), BF),
        ((512, HD), BF),
        ((512, HD), BF),
        ((512, HD), BF),
        ((NY * TOK, 1024), F32),
        ((NY * TOK, 1024), BF),
        ((NY * TOK, 512), BF),
        ((HD, NY * TOK), BF),
        ((HD, NY * TOK), BF),
        ((8, 2, NY, ROUNDS, 16, TOK), BF),
        ((NP * NY, ROUNDS, 16, TOK), BF),
        ((NP, NY, 16, TOK), BF),
        ((8, 2, NY, 16, TOK), BF),
        ((2, NY, HD, TOK), F32),
        ((2, 2, 8, 32, HD), F32),
        ((2, 8, 32, HD), BF),
        ((2, 8, 32, HD), BF),
        ((2, 8, 32, HD), BF),
        ((2, 8, 32, HD), BF),
        ((32, HD), BF),
        ((2, NY, TOK, HD), BF),
        ((2, NY, TOK, HD), BF),
    ]
    results = pl.pallas_call(
        kernel,
        out_shape=(out,) * 4,
        in_specs=[smem] * 3 + [hbm] * 4,
        out_specs=(hbm,) * 4,
        scratch_shapes=[pltpu.VMEM(*s) for s in shapes]
        + [dma((4,)), dma, dma((2, NY)), dma((2,)), dma, dma((2, NY)), dma((2,)), dma, dma((2, NY)), dma((2, 2)), dma((4,))]
        + [dma] * 5
        + [dma((2,)), dma, dma, dma((2,)), dma, dma],
        compiler_params=pltpu.CompilerParams(
            collective_id=0, has_side_effects=True, vmem_limit_bytes=63 * 1024 * 1024
        ),
        cost_estimate=pl.CostEstimate(flops=1_700_000_000, bytes_accessed=2_000_000, transcendentals=1_048_576),
    )(matches, active.reshape(ROUNDS), global_pos, queries, key_rows, value_rows, cotangent)
    return pl.pallas_call(
        hand_out,
        out_shape=(out,) * 4,
        in_specs=[hbm] * 4,
        out_specs=(hbm,) * 4,
        scratch_shapes=[pltpu.VMEM((4, TOK, NY * HD), BF), dma((2, 4))],
        compiler_params=pltpu.CompilerParams(vmem_limit_bytes=63 * 1024 * 1024),
    )(*results)


def solution(mesh):
    rows = P(("batch", "seq"), None)
    return jax.shard_map(
        local,
        mesh=mesh,
        in_specs=(rows, rows, rows, rows, P("batch", None), P("batch", "seq"), P(("batch", "seq"))),
        out_specs=(rows,) * 4,
        check_vma=False,
    )
```

```python
import jax
import jax.numpy as jnp
from jax import lax
from jax.experimental import pallas as pl
from jax.experimental.pallas import tpu as pltpu
from jax.sharding import PartitionSpec as P

HD = 128
ROUNDS = 3
NY = 8
NP = 16
EARLY = 4
TOK = 128
SCALE = HD**-0.5
LOG2E = 1.4426950408889634
BF = jnp.bfloat16
F32 = jnp.float32


def mm(a, b):
    return lax.dot_general(a, b, (((1,), (0,)), ((), ())), preferred_element_type=F32)


def mm_t(a, b):
    return lax.dot_general(a, b, (((1,), (1,)), ((), ())), preferred_element_type=F32)


def kernel(
    matches, active, gpos, q_in, k_in, v_in, g_in,
    o_out, dq_out, dk_out, dv_out,
    moved, aux, aux_all, kv, qg, inter, stage, part, gl_mine, gl_all,
    k_loc, k_glob, v_loc, v_glob, probs, low, sgrad, q_t, g_t,
    ret_stage, ret, tot_stage, tot, own, gg_stage, gg_half, gg_pair, gg_sum, gg, gsum, od_stage, kvg_stage,
    sem_moved, sem_aux, sem_kv, sem_qg, sem_inter, sem_part, sem_gl, sem_ret, sem_tot, sem_gg, sem_out,
    send_aux, send_kv, send_qg, send_inter, send_part, send_gl, send_ret, send_tot, send_gg, send_od, send_kvg,
):
    me = lax.axis_index("seq")
    my_x, my_y, my_zc = me // 32, (me // 4) % NY, me % 4
    my_z, my_core = my_zc // 2, my_zc % 2
    my_p = my_x * 4 + my_zc
    my_chip = my_p // 2

    def shard(p, y):
        return (p // 4) * 32 + y * 4 + p % 4

    def line(y):
        return {"seq": shard(my_p, y)}

    def plane(p):
        return {"seq": shard(p, my_y)}

    def line_step(n):
        return (n + 1) // 2 * (1 - 2 * ((n + 1) % 2))

    def line_to(n):
        return (my_y + NY + line_step(n)) % NY

    def line_from(n):
        return (my_y + NY - line_step(n)) % NY

    def at(x_off, zc_off):
        return (my_x + x_off) % 4 * 4 + (my_zc + zc_off) % 4

    def each_other(do):
        @pl.loop(0, 4)
        def _(i):
            do(at(2, i))

        @pl.loop(0, 4)
        def _(i):
            do(at(1, i))
            do(at(3, i))

        @pl.loop(1, 4)
        def _(i):
            do(at(0, i))

    def each_chip(do):
        @pl.loop(0, 2)
        def _(i):
            for x_off in (2, 1, 3):
                do((my_x + x_off) % 4 * 2 + (my_z + 1 + i) % 2)

        do(my_x * 2 + 1 - my_z)

    def turn(n):
        return line_to((n + 1) % NY)

    def far(n):
        return line_to(NY - 1 - n)

    def put(src, dst, send, recv, where):
        pltpu.make_async_remote_copy(
            src_ref=src, dst_ref=dst, send_sem=send, recv_sem=recv, device_id=where,
            device_id_type=pl.DeviceIdType.MESH,
        ).start()

    def keep(src, dst, recv):
        pltpu.make_async_copy(src, dst, recv).start()

    def wait(ref, sem):
        pltpu.make_async_copy(ref, ref, sem).wait()

    def cols(ref, y):
        return ref.at[:, pl.ds(pl.multiple_of(y * HD, HD), HD)]

    def to_keepers(which, src, dst, send, recv):
        each_chip(lambda tile: put(src(tile), dst, send, recv, plane(tile * 2 + which)))

        @pl.when(my_core == which)
        def _():
            keep(src(my_chip), dst, recv)

        @pl.when(my_core != which)
        def _():
            put(src(my_chip), dst, send, recv, plane(my_chip * 2 + which))

    barrier = pltpu.get_barrier_semaphore()

    @pl.loop(1, NY)
    def _(n):
        pl.semaphore_signal(barrier, inc=1, device_id=line(line_to(n)), device_id_type=pl.DeviceIdType.MESH)

    each_other(
        lambda p: pl.semaphore_signal(barrier, inc=1, device_id=plane(p), device_id_type=pl.DeviceIdType.MESH)
    )

    for n, ref in enumerate((k_in, v_in, q_in, g_in)):

        @pl.loop(0, NY)
        def _(y):
            keep(cols(ref, y), moved.at[n, y], sem_moved.at[n])

    row = lax.broadcasted_iota(jnp.int32, (32, TOK), 0)
    lane = lax.broadcasted_iota(jnp.int32, (32, TOK), 1)
    tile = jnp.zeros((32, TOK), F32)
    for n in range(4):
        here = (row == (my_y % 4) * 4 + n) & (lane == gpos[n] - me * TOK)
        tile = jnp.where(here, 1.0, tile)
    for r in range(ROUNDS):
        tile = jnp.where(row == 16 + r, active[r].astype(F32), tile)
    aux[...] = tile.astype(BF)
    for n in range(4):
        wait(moved.at[n], sem_moved.at[n])

    pl.semaphore_wait(barrier, NY - 1 + NP - 1)

    @pl.loop(1, NY)
    def _(n):
        put(moved.at[0, line_to(n)], kv.at[0, my_y], send_kv, sem_kv.at[0, my_y], line(line_to(n)))

    keep(moved.at[0, my_y], kv.at[0, my_y], sem_kv.at[0, my_y])
    keep(moved.at[1, my_y], kv.at[1, my_y], sem_kv.at[1, my_y])
    keep(moved.at[2, my_y], qg.at[0, my_y], sem_qg.at[0])
    keep(moved.at[3, my_y], qg.at[1, my_y], sem_qg.at[1])
    keep(aux, aux_all.at[my_y], sem_aux)

    @pl.loop(1, NY)
    def _(n):
        put(aux, aux_all.at[my_y], send_aux, sem_aux, line(line_to(n)))

    def hand_on(which, t):
        wait(kv.at[which, t], sem_kv.at[which, t])
        to_keepers(
            which,
            lambda tile: kv.at[which, t, pl.ds(pl.multiple_of(tile * 16, 16), 16), :],
            inter.at[shard(my_p, t)], send_inter, sem_inter,
        )

    def pick_and_send():
        wait(inter, sem_inter)

        @pl.loop(0, NY)
        def _(n):
            named = [[matches[r, shard(p, turn(n))] for r in range(ROUNDS)] for p in range(NP)]
            for p in range(NP):
                for r in range(ROUNDS):
                    stage[p, n, r] = inter[named[p][r]]

            dst, sem = part.at[my_chip, my_core, n], sem_part.at[my_core, n]

            each_other(lambda p: put(stage.at[p, n], dst, send_part, sem, plane(p)))
            keep(stage.at[my_p, n], dst, sem)

    @pl.loop(0, NY)
    def _(n):
        hand_on(0, line_from(n))

        @pl.when(n > 0)
        def _():
            put(moved.at[1, line_to(n)], kv.at[1, my_y], send_kv, sem_kv.at[1, my_y], line(line_to(n)))

    @pl.loop(0, 4)
    def _(n):
        hand_on(1, line_from(n))

        @pl.when(n > 0)
        def _():
            put(moved.at[2, line_to(n)], qg.at[0, my_y], send_qg, sem_qg.at[0], line(line_to(n)))

    @pl.when(my_core == 0)
    def _():
        pick_and_send()

    @pl.loop(4, NY)
    def _(n):
        hand_on(1, line_from(n))
        put(moved.at[2, line_to(n)], qg.at[0, my_y], send_qg, sem_qg.at[0], line(line_to(n)))

    @pl.loop(1, NY)
    def _(n):
        put(moved.at[3, line_to(n)], qg.at[1, my_y], send_qg, sem_qg.at[1], line(line_to(n)))

    wait(aux_all, sem_aux)
    for half in range(2):
        picks = jnp.concatenate([aux_all[half * 4 + n, :16] for n in range(4)], axis=1)
        for which in range(2):
            rows = kv[which, half * 4 : half * 4 + 4].reshape(4 * TOK, HD)
            gl_mine[which, half * 16 : half * 16 + 16] = mm(picks, rows).astype(BF)
    keep(gl_mine, gl_all.at[my_core, my_chip], sem_gl.at[0])

    each_chip(
        lambda chip: put(
            gl_mine, gl_all.at[my_core, my_chip], send_gl.at[0], sem_gl.at[0], plane(chip * 2 + my_core)
        )
    )

    @pl.when(my_core == 1)
    def _():
        pick_and_send()

    wait(gl_all.at[0], sem_gl.at[0])
    put(gl_all.at[my_core], gl_all.at[my_core], send_gl.at[1], sem_gl.at[1], plane(my_p + 1 - 2 * my_core))
    wait(gl_all.at[0], sem_gl.at[1])
    k_glob[...] = gl_all[:, :, 0].reshape(512, HD)
    v_glob[...] = gl_all[:, :, 1].reshape(512, HD)
    wait(qg.at[0], sem_qg.at[0])

    @pl.loop(0, NY)
    def _(n):
        t = turn(n)
        wait(part.at[:, 0, n], sem_part.at[0, n])
        q = qg[0, t]
        k_loc[t, 0:TOK] = kv[0, t]
        for r in range(ROUNDS):
            k_loc[t, TOK * (r + 1) : TOK * (r + 2)] = part[:, 0, n, r].reshape(TOK, HD)
        flags = aux_all[t, 16:32].astype(F32)
        bias = jnp.concatenate(
            [jnp.zeros((1, TOK), F32)] + [(flags[r : r + 1] - 1.0) * 1e30 for r in range(ROUNDS)], axis=1
        )
        s_loc = mm_t(q, k_loc[t]) * (SCALE * LOG2E) + bias
        s_glob = mm_t(q, k_glob[...]) * (SCALE * LOG2E)
        peak = jnp.maximum(jnp.max(s_loc, axis=1, keepdims=True), jnp.max(s_glob, axis=1, keepdims=True))
        w_loc, w_glob = jnp.exp2(s_loc - peak), jnp.exp2(s_glob - peak)
        inverse = 1.0 / (jnp.sum(w_loc, axis=1, keepdims=True) + jnp.sum(w_glob, axis=1, keepdims=True))
        p_loc, p_glob = w_loc * inverse, w_glob * inverse
        rows = pl.ds(pl.multiple_of(t * TOK, TOK), TOK)
        probs[rows, :512] = p_loc
        probs[rows, 512:] = p_glob
        low[rows, :512] = p_loc.astype(BF)
        low[rows, 512:] = p_glob.astype(BF)

    def send_back(which, t):
        to_keepers(which, lambda tile: ret_stage.at[tile, which, t], ret.at[shard(my_p, t)], send_ret, sem_ret)

    def set_terms(which, t, term):
        own[which, t] = term[:, :TOK]
        for r in range(ROUNDS):
            ret_stage[:, which, t, r] = term[:, TOK * (r + 1) : TOK * (r + 2)].astype(BF).reshape(8, 16, TOK)

    def share_globals(which, term):
        gg_stage[which] = term.T.reshape(2, 8, 32, HD)
        gg_half[which] = gg_stage[which, 1 - my_core].astype(BF)
        put(
            gg_half.at[which], gg_pair.at[which], send_gg.at[0], sem_gg.at[0, which], plane(my_p + 1 - 2 * my_core)
        )

    def give_globals(which):
        wait(gg_pair.at[which], sem_gg.at[0, which])
        gg_sum[which] = (gg_stage[which, my_core] + gg_pair[which].astype(F32)).astype(BF)
        keep(gg_sum.at[which, my_chip], gg.at[which, my_chip], sem_gg.at[1, which])

        each_chip(
            lambda chip: put(
                gg_sum.at[which, chip], gg.at[which, my_chip], send_gg.at[1], sem_gg.at[1, which],
                plane(chip * 2 + my_core),
            )
        )

    wait(qg.at[1], sem_qg.at[1])

    @pl.loop(0, NY)
    def _(t):
        rows = pl.ds(pl.multiple_of(t * TOK, TOK), TOK)
        gt = qg[1, t].T
        g_t[:, rows] = gt
        set_terms(1, t, mm(gt, low[rows, :512]))
        send_back(1, t)

    share_globals(1, mm(g_t[...], low[:, 512:]))

    @pl.loop(0, NY)
    def _(n):
        t = turn(n)
        wait(part.at[:, 1, n], sem_part.at[1, n])
        rows = pl.ds(pl.multiple_of(t * TOK, TOK), TOK)
        q, g = qg[0, t], qg[1, t]
        v_loc[0:TOK] = kv[1, t]
        for r in range(ROUNDS):
            v_loc[TOK * (r + 1) : TOK * (r + 2)] = part[:, 1, n, r].reshape(TOK, HD)
        gp_loc, gp_glob = mm_t(g, v_loc[...]), mm_t(g, v_glob[...])
        low_loc, low_glob = low[rows, :512], low[rows, 512:]
        centre = jnp.sum(low_loc.astype(F32) * gp_loc, axis=1, keepdims=True) + jnp.sum(
            low_glob.astype(F32) * gp_glob, axis=1, keepdims=True
        )
        sg_loc = (probs[rows, :512] * (gp_loc - centre)).astype(BF)
        sg_glob = (probs[rows, 512:] * (gp_glob - centre)).astype(BF)
        sgrad[rows] = sg_glob
        qt = q.T
        q_t[:, rows] = qt
        set_terms(0, t, mm(qt, sg_loc) * SCALE)

        @pl.when(n < EARLY)
        def _():
            send_back(0, t)

        od_stage[0, t] = (mm(low_loc, v_loc[...]) + mm(low_glob, v_glob[...])).astype(BF)
        od_stage[1, t] = ((mm(sg_loc, k_loc[t]) + mm(sg_glob, k_glob[...])) * SCALE).astype(BF)

        @pl.when(n == NY - 1)
        def _():
            keep(od_stage.at[0, t], cols(o_out, my_y), sem_out.at[0])
            keep(od_stage.at[1, t], cols(dq_out, my_y), sem_out.at[1])

        @pl.when(n < NY - 1)
        def _():
            put(od_stage.at[0, t], cols(o_out, my_y), send_od, sem_out.at[0], line(t))
            put(od_stage.at[1, t], cols(dq_out, my_y), send_od, sem_out.at[1], line(t))

    def add_and_send():
        wait(ret, sem_ret)

        @pl.loop(0, NY)
        def _(n):
            t = far(n)
            dst, sem = tot.at[my_p // 2, my_core, t], sem_tot.at[my_core, t]

            named = [[matches[r, shard(p, t)] for r in range(ROUNDS)] for p in range(NP)]
            for p in range(NP):
                terms = [ret[named[p][r], r].astype(F32) for r in range(ROUNDS)]
                tot_stage[p, t] = (terms[0] + terms[1] + terms[2]).astype(BF)

            each_other(lambda p: put(tot_stage.at[p, t], dst, send_tot, sem, plane(p)))
            keep(tot_stage.at[my_p, t], dst, sem)

    def finish(which, out):
        wait(gg.at[which], sem_gg.at[1, which])
        gsum[...] = jnp.sum(gg[which].astype(F32), axis=0).astype(BF)

        @pl.loop(0, NY)
        def _(n):
            t = far(n)
            wait(tot.at[:, which, t], sem_tot.at[which, t])
            rows = gsum[pl.ds(pl.multiple_of((t // 4) * 16, 16), 16)]
            back = own[which, t] + tot[:, which, t].reshape(HD, TOK).astype(F32)
            there = lax.dot_general(aux_all[t, :16], rows, (((0,), (0,)), ((), ())), preferred_element_type=F32)
            kvg_stage[which, t] = (back.T + there).astype(BF)

            @pl.when(n == NY - 1)
            def _():
                keep(kvg_stage.at[which, t], cols(out, my_y), sem_out.at[2 + which])

            @pl.when(n < NY - 1)
            def _():
                put(kvg_stage.at[which, t], cols(out, my_y), send_kvg, sem_out.at[2 + which], line(t))

    give_globals(1)

    @pl.when(my_core == 1)
    def _():
        add_and_send()

    @pl.loop(EARLY, NY)
    def _(n):
        send_back(0, turn(n))

    share_globals(0, mm(q_t[...], sgrad[...]) * SCALE)
    give_globals(0)
    finish(1, dv_out)

    @pl.when(my_core == 0)
    def _():
        add_and_send()

    finish(0, dk_out)

    for n, out in enumerate((o_out, dq_out, dk_out, dv_out)):
        wait(out, sem_out.at[n])
    wait(aux_all.at[: NY - 1], send_aux)
    for sem in (send_kv, send_qg, send_od, send_kvg):
        wait(kv.at[:, : NY - 1], sem)
    for sem in (send_inter, send_tot):
        wait(tot_stage.at[: NP - 1], sem)
    for sem in (send_part, send_ret):
        wait(stage.at[: NP - 1], sem)
    wait(gl_all.at[0, :7], send_gl.at[0])
    wait(gl_all.at[0], send_gl.at[1])
    wait(gg_half, send_gg.at[0])
    wait(gg.at[:, :7], send_gg.at[1])


def hand_out(*refs):
    ins, outs, held, sems = refs[:4], refs[4:8], refs[8], refs[9]
    come = [pltpu.make_async_copy(a, held.at[n], sems.at[0, n]) for n, a in enumerate(ins)]
    go = [pltpu.make_async_copy(held.at[n], b, sems.at[1, n]) for n, b in enumerate(outs)]
    for copy in come:
        copy.start()
    for n in range(4):
        come[n].wait()
        go[n].start()
    for copy in go:
        copy.wait()


def local(queries, key_rows, value_rows, cotangent, matches, active, global_pos):
    out = jax.ShapeDtypeStruct(queries.shape, BF)
    smem, hbm = (pl.BlockSpec(memory_space=m) for m in (pltpu.SMEM, pltpu.HBM))
    dma = pltpu.SemaphoreType.DMA
    shapes = [
        ((4, NY, TOK, HD), BF),
        ((32, TOK), BF),
        ((NY, 32, TOK), BF),
        ((2, NY, TOK, HD), BF),
        ((2, NY, TOK, HD), BF),
        ((NP * NY, 16, HD), BF),
        ((NP, NY, ROUNDS, 16, HD), BF),
        ((8, 2, NY, ROUNDS, 16, HD), BF),
        ((2, 32, HD), BF),
        ((2, 8, 2, 32, HD), BF),
        ((NY, 512, HD), BF),
        ((512, HD), BF),
        ((512, HD), BF),
        ((512, HD), BF),
        ((NY * TOK, 1024), F32),
        ((NY * TOK, 1024), BF),
        ((NY * TOK, 512), BF),
        ((HD, NY * TOK), BF),
        ((HD, NY * TOK), BF),
        ((8, 2, NY, ROUNDS, 16, TOK), BF),
        ((NP * NY, ROUNDS, 16, TOK), BF),
        ((NP, NY, 16, TOK), BF),
        ((8, 2, NY, 16, TOK), BF),
        ((2, NY, HD, TOK), F32),
        ((2, 2, 8, 32, HD), F32),
        ((2, 8, 32, HD), BF),
        ((2, 8, 32, HD), BF),
        ((2, 8, 32, HD), BF),
        ((2, 8, 32, HD), BF),
        ((32, HD), BF),
        ((2, NY, TOK, HD), BF),
        ((2, NY, TOK, HD), BF),
    ]
    results = pl.pallas_call(
        kernel,
        out_shape=(out,) * 4,
        in_specs=[smem] * 3 + [hbm] * 4,
        out_specs=(hbm,) * 4,
        scratch_shapes=[pltpu.VMEM(*s) for s in shapes]
        + [dma((4,)), dma, dma((2, NY)), dma((2,)), dma, dma((2, NY)), dma((2,)), dma, dma((2, NY)), dma((2, 2)), dma((4,))]
        + [dma] * 5
        + [dma((2,)), dma, dma, dma((2,)), dma, dma],
        compiler_params=pltpu.CompilerParams(
            collective_id=0, has_side_effects=True, vmem_limit_bytes=63 * 1024 * 1024
        ),
        cost_estimate=pl.CostEstimate(flops=1_700_000_000, bytes_accessed=2_000_000, transcendentals=1_048_576),
    )(matches, active.reshape(ROUNDS), global_pos, queries, key_rows, value_rows, cotangent)
    return pl.pallas_call(
        hand_out,
        out_shape=(out,) * 4,
        in_specs=[hbm] * 4,
        out_specs=(hbm,) * 4,
        scratch_shapes=[pltpu.VMEM((4, TOK, NY * HD), BF), dma((2, 4))],
        compiler_params=pltpu.CompilerParams(vmem_limit_bytes=63 * 1024 * 1024),
    )(*results)


def solution(mesh):
    rows = P(("batch", "seq"), None)
    return jax.shard_map(
        local,
        mesh=mesh,
        in_specs=(rows, rows, rows, rows, P("batch", None), P("batch", "seq"), P(("batch", "seq"))),
        out_specs=(rows,) * 4,
        check_vma=False,
    )
```

```python
import jax
import jax.numpy as jnp
from jax import lax
from jax.experimental import pallas as pl
from jax.experimental.pallas import tpu as pltpu
from jax.sharding import PartitionSpec as P

HD = 128
ROUNDS = 3
NY = 8
NP = 16
EARLY = 3
TOK = 128
SCALE = HD**-0.5
LOG2E = 1.4426950408889634
BF = jnp.bfloat16
F32 = jnp.float32


def mm(a, b):
    return lax.dot_general(a, b, (((1,), (0,)), ((), ())), preferred_element_type=F32)


def mm_t(a, b):
    return lax.dot_general(a, b, (((1,), (1,)), ((), ())), preferred_element_type=F32)


def kernel(
    matches, active, gpos, q_in, k_in, v_in, g_in,
    o_out, dq_out, dk_out, dv_out,
    moved, aux, aux_all, kv, qg, inter, stage, part, gl_mine, gl_all,
    k_loc, k_glob, v_loc, v_glob, probs, low, sgrad, q_t, g_t,
    ret_stage, ret, tot_stage, tot, own, gg_stage, gg_half, gg_pair, gg_sum, gg, gsum, od_stage, kvg_stage,
    sem_moved, sem_aux, sem_kv, sem_qg, sem_inter, sem_part, sem_gl, sem_ret, sem_tot, sem_gg, sem_out,
    send_aux, send_kv, send_qg, send_inter, send_part, send_gl, send_ret, send_tot, send_gg, send_od, send_kvg,
):
    me = lax.axis_index("seq")
    my_x, my_y, my_zc = me // 32, (me // 4) % NY, me % 4
    my_z, my_core = my_zc // 2, my_zc % 2
    my_p = my_x * 4 + my_zc
    my_chip = my_p // 2

    def shard(p, y):
        return (p // 4) * 32 + y * 4 + p % 4

    def line(y):
        return {"seq": shard(my_p, y)}

    def plane(p):
        return {"seq": shard(p, my_y)}

    def line_step(n):
        return (n + 1) // 2 * (1 - 2 * ((n + 1) % 2))

    def line_to(n):
        return (my_y + NY + line_step(n)) % NY

    def line_from(n):
        return (my_y + NY - line_step(n)) % NY

    def at(x_off, zc_off):
        return (my_x + x_off) % 4 * 4 + (my_zc + zc_off) % 4

    def each_other(do):
        @pl.loop(0, 4)
        def _(i):
            do(at(2, i))

        @pl.loop(0, 4)
        def _(i):
            do(at(1, i))
            do(at(3, i))

        @pl.loop(1, 4)
        def _(i):
            do(at(0, i))

    def each_chip(do):
        @pl.loop(0, 2)
        def _(i):
            for x_off in (2, 1, 3):
                do((my_x + x_off) % 4 * 2 + (my_z + 1 + i) % 2)

        do(my_x * 2 + 1 - my_z)

    def turn(n):
        return line_to((n + 1) % NY)

    def far(n):
        return line_to(NY - 1 - n)

    def put(src, dst, send, recv, where):
        pltpu.make_async_remote_copy(
            src_ref=src, dst_ref=dst, send_sem=send, recv_sem=recv, device_id=where,
            device_id_type=pl.DeviceIdType.MESH,
        ).start()

    def keep(src, dst, recv):
        pltpu.make_async_copy(src, dst, recv).start()

    def wait(ref, sem):
        pltpu.make_async_copy(ref, ref, sem).wait()

    def cols(ref, y):
        return ref.at[:, pl.ds(pl.multiple_of(y * HD, HD), HD)]

    def to_keepers(which, src, dst, send, recv):
        each_chip(lambda tile: put(src(tile), dst, send, recv, plane(tile * 2 + which)))

        @pl.when(my_core == which)
        def _():
            keep(src(my_chip), dst, recv)

        @pl.when(my_core != which)
        def _():
            put(src(my_chip), dst, send, recv, plane(my_chip * 2 + which))

    barrier = pltpu.get_barrier_semaphore()

    @pl.loop(1, NY)
    def _(n):
        pl.semaphore_signal(barrier, inc=1, device_id=line(line_to(n)), device_id_type=pl.DeviceIdType.MESH)

    each_other(
        lambda p: pl.semaphore_signal(barrier, inc=1, device_id=plane(p), device_id_type=pl.DeviceIdType.MESH)
    )

    for n, ref in enumerate((k_in, v_in, q_in, g_in)):

        @pl.loop(0, NY)
        def _(y):
            keep(cols(ref, y), moved.at[n, y], sem_moved.at[n])

    wait(moved.at[0], sem_moved.at[0])
    pl.semaphore_wait(barrier, NY - 1 + NP - 1)

    @pl.loop(1, NY)
    def _(n):
        put(moved.at[0, line_to(n)], kv.at[0, my_y], send_kv, sem_kv.at[0, my_y], line(line_to(n)))

    row = lax.broadcasted_iota(jnp.int32, (32, TOK), 0)
    lane = lax.broadcasted_iota(jnp.int32, (32, TOK), 1)
    tile = jnp.zeros((32, TOK), F32)
    for n in range(4):
        here = (row == (my_y % 4) * 4 + n) & (lane == gpos[n] - me * TOK)
        tile = jnp.where(here, 1.0, tile)
    for r in range(ROUNDS):
        tile = jnp.where(row == 16 + r, active[r].astype(F32), tile)
    aux[...] = tile.astype(BF)
    for n in range(1, 4):
        wait(moved.at[n], sem_moved.at[n])

    keep(moved.at[0, my_y], kv.at[0, my_y], sem_kv.at[0, my_y])
    keep(moved.at[1, my_y], kv.at[1, my_y], sem_kv.at[1, my_y])
    keep(moved.at[2, my_y], qg.at[0, my_y], sem_qg.at[0])
    keep(moved.at[3, my_y], qg.at[1, my_y], sem_qg.at[1])
    keep(aux, aux_all.at[my_y], sem_aux)

    def hand_on(which, t):
        wait(kv.at[which, t], sem_kv.at[which, t])
        to_keepers(
            which,
            lambda tile: kv.at[which, t, pl.ds(pl.multiple_of(tile * 16, 16), 16), :],
            inter.at[shard(my_p, t)], send_inter, sem_inter,
        )

    def pick_and_send():
        wait(inter, sem_inter)

        @pl.loop(0, NY)
        def _(n):
            named = [[matches[r, shard(p, turn(n))] for r in range(ROUNDS)] for p in range(NP)]
            for p in range(NP):
                for r in range(ROUNDS):
                    stage[p, n, r] = inter[named[p][r]]

            dst, sem = part.at[my_chip, my_core, n], sem_part.at[my_core, n]

            each_other(lambda p: put(stage.at[p, n], dst, send_part, sem, plane(p)))
            keep(stage.at[my_p, n], dst, sem)

    @pl.loop(0, NY)
    def _(n):
        hand_on(0, line_from(n))

        @pl.when(n > 0)
        def _():
            put(moved.at[1, line_to(n)], kv.at[1, my_y], send_kv, sem_kv.at[1, my_y], line(line_to(n)))

    @pl.loop(1, NY)
    def _(n):
        put(aux, aux_all.at[my_y], send_aux, sem_aux, line(line_to(n)))

    @pl.loop(0, 4)
    def _(n):
        hand_on(1, line_from(n))

        @pl.when(n > 0)
        def _():
            put(moved.at[2, line_to(n)], qg.at[0, my_y], send_qg, sem_qg.at[0], line(line_to(n)))

    @pl.when(my_core == 0)
    def _():
        pick_and_send()

    @pl.loop(4, NY)
    def _(n):
        hand_on(1, line_from(n))
        put(moved.at[2, line_to(n)], qg.at[0, my_y], send_qg, sem_qg.at[0], line(line_to(n)))

    @pl.loop(1, NY)
    def _(n):
        put(moved.at[3, line_to(n)], qg.at[1, my_y], send_qg, sem_qg.at[1], line(line_to(n)))

    wait(aux_all, sem_aux)
    for half in range(2):
        picks = jnp.concatenate([aux_all[half * 4 + n, :16] for n in range(4)], axis=1)
        for which in range(2):
            rows = kv[which, half * 4 : half * 4 + 4].reshape(4 * TOK, HD)
            gl_mine[which, half * 16 : half * 16 + 16] = mm(picks, rows).astype(BF)
    keep(gl_mine, gl_all.at[my_core, my_chip], sem_gl.at[0])

    each_chip(
        lambda chip: put(
            gl_mine, gl_all.at[my_core, my_chip], send_gl.at[0], sem_gl.at[0], plane(chip * 2 + my_core)
        )
    )

    @pl.when(my_core == 1)
    def _():
        pick_and_send()

    wait(gl_all.at[0], sem_gl.at[0])
    put(gl_all.at[my_core], gl_all.at[my_core], send_gl.at[1], sem_gl.at[1], plane(my_p + 1 - 2 * my_core))
    wait(gl_all.at[0], sem_gl.at[1])
    k_glob[...] = gl_all[:, :, 0].reshape(512, HD)
    v_glob[...] = gl_all[:, :, 1].reshape(512, HD)
    wait(qg.at[0], sem_qg.at[0])

    @pl.loop(0, NY)
    def _(n):
        t = turn(n)
        wait(part.at[:, 0, n], sem_part.at[0, n])
        q = qg[0, t]
        k_loc[t, 0:TOK] = kv[0, t]
        for r in range(ROUNDS):
            k_loc[t, TOK * (r + 1) : TOK * (r + 2)] = part[:, 0, n, r].reshape(TOK, HD)
        flags = aux_all[t, 16:32].astype(F32)
        bias = jnp.concatenate(
            [jnp.zeros((1, TOK), F32)] + [(flags[r : r + 1] - 1.0) * 1e30 for r in range(ROUNDS)], axis=1
        )
        s_loc = mm_t(q, k_loc[t]) * (SCALE * LOG2E) + bias
        s_glob = mm_t(q, k_glob[...]) * (SCALE * LOG2E)
        peak = jnp.maximum(jnp.max(s_loc, axis=1, keepdims=True), jnp.max(s_glob, axis=1, keepdims=True))
        w_loc, w_glob = jnp.exp2(s_loc - peak), jnp.exp2(s_glob - peak)
        inverse = 1.0 / (jnp.sum(w_loc, axis=1, keepdims=True) + jnp.sum(w_glob, axis=1, keepdims=True))
        p_loc, p_glob = w_loc * inverse, w_glob * inverse
        rows = pl.ds(pl.multiple_of(t * TOK, TOK), TOK)
        probs[rows, :512] = p_loc
        probs[rows, 512:] = p_glob
        low[rows, :512] = p_loc.astype(BF)
        low[rows, 512:] = p_glob.astype(BF)

    def send_back(which, t):
        to_keepers(which, lambda tile: ret_stage.at[tile, which, t], ret.at[shard(my_p, t)], send_ret, sem_ret)

    def set_terms(which, t, term):
        own[which, t] = term[:, :TOK]
        for r in range(ROUNDS):
            ret_stage[:, which, t, r] = term[:, TOK * (r + 1) : TOK * (r + 2)].astype(BF).reshape(8, 16, TOK)

    def share_globals(which, term):
        gg_stage[which] = term.T.reshape(2, 8, 32, HD)
        gg_half[which] = gg_stage[which, 1 - my_core].astype(BF)
        put(
            gg_half.at[which], gg_pair.at[which], send_gg.at[0], sem_gg.at[0, which], plane(my_p + 1 - 2 * my_core)
        )

    def give_globals(which):
        wait(gg_pair.at[which], sem_gg.at[0, which])
        gg_sum[which] = (gg_stage[which, my_core] + gg_pair[which].astype(F32)).astype(BF)
        keep(gg_sum.at[which, my_chip], gg.at[which, my_chip], sem_gg.at[1, which])

        each_chip(
            lambda chip: put(
                gg_sum.at[which, chip], gg.at[which, my_chip], send_gg.at[1], sem_gg.at[1, which],
                plane(chip * 2 + my_core),
            )
        )

    wait(qg.at[1], sem_qg.at[1])

    @pl.loop(0, NY)
    def _(t):
        rows = pl.ds(pl.multiple_of(t * TOK, TOK), TOK)
        gt = qg[1, t].T
        g_t[:, rows] = gt
        set_terms(1, t, mm(gt, low[rows, :512]))
        send_back(1, t)

    share_globals(1, mm(g_t[...], low[:, 512:]))

    @pl.loop(0, NY)
    def _(n):
        t = turn(n)
        wait(part.at[:, 1, n], sem_part.at[1, n])
        rows = pl.ds(pl.multiple_of(t * TOK, TOK), TOK)
        q, g = qg[0, t], qg[1, t]
        v_loc[0:TOK] = kv[1, t]
        for r in range(ROUNDS):
            v_loc[TOK * (r + 1) : TOK * (r + 2)] = part[:, 1, n, r].reshape(TOK, HD)
        gp_loc, gp_glob = mm_t(g, v_loc[...]), mm_t(g, v_glob[...])
        low_loc, low_glob = low[rows, :512], low[rows, 512:]
        centre = jnp.sum(low_loc.astype(F32) * gp_loc, axis=1, keepdims=True) + jnp.sum(
            low_glob.astype(F32) * gp_glob, axis=1, keepdims=True
        )
        sg_loc = (probs[rows, :512] * (gp_loc - centre)).astype(BF)
        sg_glob = (probs[rows, 512:] * (gp_glob - centre)).astype(BF)
        sgrad[rows] = sg_glob
        qt = q.T
        q_t[:, rows] = qt
        set_terms(0, t, mm(qt, sg_loc) * SCALE)

        @pl.when(n < EARLY)
        def _():
            send_back(0, t)

        od_stage[0, t] = (mm(low_loc, v_loc[...]) + mm(low_glob, v_glob[...])).astype(BF)
        od_stage[1, t] = ((mm(sg_loc, k_loc[t]) + mm(sg_glob, k_glob[...])) * SCALE).astype(BF)

        @pl.when(n == NY - 1)
        def _():
            keep(od_stage.at[0, t], cols(o_out, my_y), sem_out.at[0])
            keep(od_stage.at[1, t], cols(dq_out, my_y), sem_out.at[1])

        @pl.when(n < NY - 1)
        def _():
            put(od_stage.at[0, t], cols(o_out, my_y), send_od, sem_out.at[0], line(t))
            put(od_stage.at[1, t], cols(dq_out, my_y), send_od, sem_out.at[1], line(t))

    def add_and_send():
        wait(ret, sem_ret)

        @pl.loop(0, NY)
        def _(n):
            t = far(n)
            dst, sem = tot.at[my_p // 2, my_core, t], sem_tot.at[my_core, t]

            named = [[matches[r, shard(p, t)] for r in range(ROUNDS)] for p in range(NP)]
            for p in range(NP):
                terms = [ret[named[p][r], r].astype(F32) for r in range(ROUNDS)]
                tot_stage[p, t] = (terms[0] + terms[1] + terms[2]).astype(BF)

            each_other(lambda p: put(tot_stage.at[p, t], dst, send_tot, sem, plane(p)))
            keep(tot_stage.at[my_p, t], dst, sem)

    def finish(which, out):
        wait(gg.at[which], sem_gg.at[1, which])
        gsum[...] = jnp.sum(gg[which].astype(F32), axis=0).astype(BF)

        @pl.loop(0, NY)
        def _(n):
            t = far(n)
            wait(tot.at[:, which, t], sem_tot.at[which, t])
            rows = gsum[pl.ds(pl.multiple_of((t // 4) * 16, 16), 16)]
            back = own[which, t] + tot[:, which, t].reshape(HD, TOK).astype(F32)
            there = lax.dot_general(aux_all[t, :16], rows, (((0,), (0,)), ((), ())), preferred_element_type=F32)
            kvg_stage[which, t] = (back.T + there).astype(BF)

            @pl.when(n == NY - 1)
            def _():
                keep(kvg_stage.at[which, t], cols(out, my_y), sem_out.at[2 + which])

            @pl.when(n < NY - 1)
            def _():
                put(kvg_stage.at[which, t], cols(out, my_y), send_kvg, sem_out.at[2 + which], line(t))

    give_globals(1)

    @pl.when(my_core == 1)
    def _():
        add_and_send()

    @pl.loop(EARLY, NY)
    def _(n):
        send_back(0, turn(n))

    share_globals(0, mm(q_t[...], sgrad[...]) * SCALE)
    finish(1, dv_out)
    give_globals(0)

    @pl.when(my_core == 0)
    def _():
        add_and_send()

    finish(0, dk_out)

    for n, out in enumerate((o_out, dq_out, dk_out, dv_out)):
        wait(out, sem_out.at[n])
    wait(aux_all.at[: NY - 1], send_aux)
    for sem in (send_kv, send_qg, send_od, send_kvg):
        wait(kv.at[:, : NY - 1], sem)
    for sem in (send_inter, send_tot):
        wait(tot_stage.at[: NP - 1], sem)
    for sem in (send_part, send_ret):
        wait(stage.at[: NP - 1], sem)
    wait(gl_all.at[0, :7], send_gl.at[0])
    wait(gl_all.at[0], send_gl.at[1])
    wait(gg_half, send_gg.at[0])
    wait(gg.at[:, :7], send_gg.at[1])


def hand_out(*refs):
    ins, outs, held, sems = refs[:4], refs[4:8], refs[8], refs[9]
    come = [pltpu.make_async_copy(a, held.at[n], sems.at[0, n]) for n, a in enumerate(ins)]
    go = [pltpu.make_async_copy(held.at[n], b, sems.at[1, n]) for n, b in enumerate(outs)]
    for copy in come:
        copy.start()
    for n in range(4):
        come[n].wait()
        go[n].start()
    for copy in go:
        copy.wait()


def local(queries, key_rows, value_rows, cotangent, matches, active, global_pos):
    out = jax.ShapeDtypeStruct(queries.shape, BF)
    smem, hbm = (pl.BlockSpec(memory_space=m) for m in (pltpu.SMEM, pltpu.HBM))
    dma = pltpu.SemaphoreType.DMA
    shapes = [
        ((4, NY, TOK, HD), BF),
        ((32, TOK), BF),
        ((NY, 32, TOK), BF),
        ((2, NY, TOK, HD), BF),
        ((2, NY, TOK, HD), BF),
        ((NP * NY, 16, HD), BF),
        ((NP, NY, ROUNDS, 16, HD), BF),
        ((8, 2, NY, ROUNDS, 16, HD), BF),
        ((2, 32, HD), BF),
        ((2, 8, 2, 32, HD), BF),
        ((NY, 512, HD), BF),
        ((512, HD), BF),
        ((512, HD), BF),
        ((512, HD), BF),
        ((NY * TOK, 1024), F32),
        ((NY * TOK, 1024), BF),
        ((NY * TOK, 512), BF),
        ((HD, NY * TOK), BF),
        ((HD, NY * TOK), BF),
        ((8, 2, NY, ROUNDS, 16, TOK), BF),
        ((NP * NY, ROUNDS, 16, TOK), BF),
        ((NP, NY, 16, TOK), BF),
        ((8, 2, NY, 16, TOK), BF),
        ((2, NY, HD, TOK), F32),
        ((2, 2, 8, 32, HD), F32),
        ((2, 8, 32, HD), BF),
        ((2, 8, 32, HD), BF),
        ((2, 8, 32, HD), BF),
        ((2, 8, 32, HD), BF),
        ((32, HD), BF),
        ((2, NY, TOK, HD), BF),
        ((2, NY, TOK, HD), BF),
    ]
    results = pl.pallas_call(
        kernel,
        out_shape=(out,) * 4,
        in_specs=[smem] * 3 + [hbm] * 4,
        out_specs=(hbm,) * 4,
        scratch_shapes=[pltpu.VMEM(*s) for s in shapes]
        + [dma((4,)), dma, dma((2, NY)), dma((2,)), dma, dma((2, NY)), dma((2,)), dma, dma((2, NY)), dma((2, 2)), dma((4,))]
        + [dma] * 5
        + [dma((2,)), dma, dma, dma((2,)), dma, dma],
        compiler_params=pltpu.CompilerParams(
            collective_id=0, has_side_effects=True, vmem_limit_bytes=63 * 1024 * 1024
        ),
        cost_estimate=pl.CostEstimate(flops=1_700_000_000, bytes_accessed=2_000_000, transcendentals=1_048_576),
    )(matches, active.reshape(ROUNDS), global_pos, queries, key_rows, value_rows, cotangent)
    return pl.pallas_call(
        hand_out,
        out_shape=(out,) * 4,
        in_specs=[hbm] * 4,
        out_specs=(hbm,) * 4,
        scratch_shapes=[pltpu.VMEM((4, TOK, NY * HD), BF), dma((2, 4))],
        compiler_params=pltpu.CompilerParams(vmem_limit_bytes=63 * 1024 * 1024),
    )(*results)


def solution(mesh):
    rows = P(("batch", "seq"), None)
    return jax.shard_map(
        local,
        mesh=mesh,
        in_specs=(rows, rows, rows, rows, P("batch", None), P("batch", "seq"), P(("batch", "seq"))),
        out_specs=(rows,) * 4,
        check_vma=False,
    )
```

```python
import jax
import jax.numpy as jnp
from jax import lax
from jax.experimental import pallas as pl
from jax.experimental.pallas import tpu as pltpu
from jax.sharding import PartitionSpec as P

HD = 128
ROUNDS = 3
NY = 8
NP = 16
EARLY = 3
TOK = 128
SCALE = HD**-0.5
LOG2E = 1.4426950408889634
BF = jnp.bfloat16
F32 = jnp.float32


def mm(a, b):
    return lax.dot_general(a, b, (((1,), (0,)), ((), ())), preferred_element_type=F32)


def mm_t(a, b):
    return lax.dot_general(a, b, (((1,), (1,)), ((), ())), preferred_element_type=F32)


def kernel(
    matches, active, gpos, q_in, k_in, v_in, g_in,
    o_out, dq_out, dk_out, dv_out,
    moved, aux, aux_all, kv, qg, inter, stage, part, gl_mine, gl_all,
    k_loc, k_glob, v_loc, v_glob, probs, low, sgrad, q_t, g_t,
    ret_stage, ret, tot_stage, tot, own, gg_stage, gg_half, gg_pair, gg_sum, gg, gsum, od_stage, kvg_stage,
    sem_moved, sem_aux, sem_kv, sem_qg, sem_inter, sem_part, sem_gl, sem_ret, sem_tot, sem_gg, sem_out,
    send_aux, send_kv, send_qg, send_inter, send_part, send_gl, send_ret, send_tot, send_gg, send_od, send_kvg,
):
    me = lax.axis_index("seq")
    my_x, my_y, my_zc = me // 32, (me // 4) % NY, me % 4
    my_z, my_core = my_zc // 2, my_zc % 2
    my_p = my_x * 4 + my_zc
    my_chip = my_p // 2

    def shard(p, y):
        return (p // 4) * 32 + y * 4 + p % 4

    def line(y):
        return {"seq": shard(my_p, y)}

    def plane(p):
        return {"seq": shard(p, my_y)}

    def line_step(n):
        return (n + 1) // 2 * (1 - 2 * ((n + 1) % 2))

    def line_to(n):
        return (my_y + NY + line_step(n)) % NY

    def line_from(n):
        return (my_y + NY - line_step(n)) % NY

    def at(x_off, zc_off):
        return (my_x + x_off) % 4 * 4 + (my_zc + zc_off) % 4

    def each_other(do):
        @pl.loop(0, 4)
        def _(i):
            do(at(2, i))

        @pl.loop(0, 4)
        def _(i):
            do(at(1, i))
            do(at(3, i))

        @pl.loop(1, 4)
        def _(i):
            do(at(0, i))

    def each_chip(do):
        @pl.loop(0, 2)
        def _(i):
            for x_off in (2, 1, 3):
                do((my_x + x_off) % 4 * 2 + (my_z + 1 + i) % 2)

        do(my_x * 2 + 1 - my_z)

    def turn(n):
        return line_to((n + 1) % NY)

    def far(n):
        return line_to(NY - 1 - n)

    def put(src, dst, send, recv, where):
        pltpu.make_async_remote_copy(
            src_ref=src, dst_ref=dst, send_sem=send, recv_sem=recv, device_id=where,
            device_id_type=pl.DeviceIdType.MESH,
        ).start()

    def keep(src, dst, recv):
        pltpu.make_async_copy(src, dst, recv).start()

    def wait(ref, sem):
        pltpu.make_async_copy(ref, ref, sem).wait()

    def cols(ref, y):
        return ref.at[:, pl.ds(pl.multiple_of(y * HD, HD), HD)]

    def to_keepers(which, src, dst, send, recv):
        each_chip(lambda tile: put(src(tile), dst, send, recv, plane(tile * 2 + which)))

        @pl.when(my_core == which)
        def _():
            keep(src(my_chip), dst, recv)

        @pl.when(my_core != which)
        def _():
            put(src(my_chip), dst, send, recv, plane(my_chip * 2 + which))

    barrier = pltpu.get_barrier_semaphore()

    @pl.loop(1, NY)
    def _(n):
        pl.semaphore_signal(barrier, inc=1, device_id=line(line_to(n)), device_id_type=pl.DeviceIdType.MESH)

    each_other(
        lambda p: pl.semaphore_signal(barrier, inc=1, device_id=plane(p), device_id_type=pl.DeviceIdType.MESH)
    )

    for n, ref in enumerate((k_in, v_in, q_in, g_in)):

        @pl.loop(0, NY)
        def _(y):
            keep(cols(ref, y), moved.at[n, y], sem_moved.at[n])

    wait(moved.at[0], sem_moved.at[0])
    pl.semaphore_wait(barrier, NY - 1 + NP - 1)

    @pl.loop(1, NY)
    def _(n):
        put(moved.at[0, line_to(n)], kv.at[0, my_y], send_kv, sem_kv.at[0, my_y], line(line_to(n)))

    row = lax.broadcasted_iota(jnp.int32, (32, TOK), 0)
    lane = lax.broadcasted_iota(jnp.int32, (32, TOK), 1)
    tile = jnp.zeros((32, TOK), F32)
    for n in range(4):
        here = (row == (my_y % 4) * 4 + n) & (lane == gpos[n] - me * TOK)
        tile = jnp.where(here, 1.0, tile)
    for r in range(ROUNDS):
        tile = jnp.where(row == 16 + r, active[r].astype(F32), tile)
    aux[...] = tile.astype(BF)
    for n in range(1, 4):
        wait(moved.at[n], sem_moved.at[n])

    keep(moved.at[0, my_y], kv.at[0, my_y], sem_kv.at[0, my_y])
    keep(moved.at[1, my_y], kv.at[1, my_y], sem_kv.at[1, my_y])
    keep(moved.at[2, my_y], qg.at[0, my_y], sem_qg.at[0])
    keep(moved.at[3, my_y], qg.at[1, my_y], sem_qg.at[1])
    keep(aux, aux_all.at[my_y], sem_aux)

    @pl.loop(1, NY)
    def _(n):
        put(aux, aux_all.at[my_y], send_aux, sem_aux, line(line_to(n)))

    def hand_on(which, t):
        wait(kv.at[which, t], sem_kv.at[which, t])
        to_keepers(
            which,
            lambda tile: kv.at[which, t, pl.ds(pl.multiple_of(tile * 16, 16), 16), :],
            inter.at[shard(my_p, t)], send_inter, sem_inter,
        )

    def pick_and_send():
        wait(inter, sem_inter)

        @pl.loop(0, NY)
        def _(n):
            named = [[matches[r, shard(p, turn(n))] for r in range(ROUNDS)] for p in range(NP)]
            for p in range(NP):
                for r in range(ROUNDS):
                    stage[p, n, r] = inter[named[p][r]]

            dst, sem = part.at[my_chip, my_core, n], sem_part.at[my_core, n]

            each_other(lambda p: put(stage.at[p, n], dst, send_part, sem, plane(p)))
            keep(stage.at[my_p, n], dst, sem)

    @pl.loop(0, NY)
    def _(n):
        hand_on(0, line_from(n))

        @pl.when(n > 0)
        def _():
            put(moved.at[1, line_to(n)], kv.at[1, my_y], send_kv, sem_kv.at[1, my_y], line(line_to(n)))

    @pl.loop(0, 4)
    def _(n):
        hand_on(1, line_from(n))

        @pl.when(n > 0)
        def _():
            put(moved.at[2, line_to(n)], qg.at[0, my_y], send_qg, sem_qg.at[0], line(line_to(n)))

    @pl.when(my_core == 0)
    def _():
        pick_and_send()

    @pl.loop(4, NY)
    def _(n):
        hand_on(1, line_from(n))
        put(moved.at[2, line_to(n)], qg.at[0, my_y], send_qg, sem_qg.at[0], line(line_to(n)))

    @pl.loop(1, NY)
    def _(n):
        put(moved.at[3, line_to(n)], qg.at[1, my_y], send_qg, sem_qg.at[1], line(line_to(n)))

    wait(aux_all, sem_aux)
    for half in range(2):
        picks = jnp.concatenate([aux_all[half * 4 + n, :16] for n in range(4)], axis=1)
        for which in range(2):
            rows = kv[which, half * 4 : half * 4 + 4].reshape(4 * TOK, HD)
            gl_mine[which, half * 16 : half * 16 + 16] = mm(picks, rows).astype(BF)
    keep(gl_mine, gl_all.at[my_core, my_chip], sem_gl.at[0])

    each_chip(
        lambda chip: put(
            gl_mine, gl_all.at[my_core, my_chip], send_gl.at[0], sem_gl.at[0], plane(chip * 2 + my_core)
        )
    )

    @pl.when(my_core == 1)
    def _():
        pick_and_send()

    wait(gl_all.at[0], sem_gl.at[0])
    put(gl_all.at[my_core], gl_all.at[my_core], send_gl.at[1], sem_gl.at[1], plane(my_p + 1 - 2 * my_core))
    wait(gl_all.at[0], sem_gl.at[1])
    k_glob[...] = gl_all[:, :, 0].reshape(512, HD)
    v_glob[...] = gl_all[:, :, 1].reshape(512, HD)
    wait(qg.at[0], sem_qg.at[0])

    @pl.loop(0, NY)
    def _(n):
        t = turn(n)
        wait(part.at[:, 0, n], sem_part.at[0, n])
        q = qg[0, t]
        k_loc[t, 0:TOK] = kv[0, t]
        for r in range(ROUNDS):
            k_loc[t, TOK * (r + 1) : TOK * (r + 2)] = part[:, 0, n, r].reshape(TOK, HD)
        flags = aux_all[t, 16:32].astype(F32)
        bias = jnp.concatenate(
            [jnp.zeros((1, TOK), F32)] + [(flags[r : r + 1] - 1.0) * 1e30 for r in range(ROUNDS)], axis=1
        )
        s_loc = mm_t(q, k_loc[t]) * (SCALE * LOG2E) + bias
        s_glob = mm_t(q, k_glob[...]) * (SCALE * LOG2E)
        peak = jnp.maximum(jnp.max(s_loc, axis=1, keepdims=True), jnp.max(s_glob, axis=1, keepdims=True))
        w_loc, w_glob = jnp.exp2(s_loc - peak), jnp.exp2(s_glob - peak)
        inverse = 1.0 / (jnp.sum(w_loc, axis=1, keepdims=True) + jnp.sum(w_glob, axis=1, keepdims=True))
        p_loc, p_glob = w_loc * inverse, w_glob * inverse
        rows = pl.ds(pl.multiple_of(t * TOK, TOK), TOK)
        probs[rows, :512] = p_loc
        probs[rows, 512:] = p_glob
        low[rows, :512] = p_loc.astype(BF)
        low[rows, 512:] = p_glob.astype(BF)

    def send_back(which, t):
        to_keepers(which, lambda tile: ret_stage.at[tile, which, t], ret.at[shard(my_p, t)], send_ret, sem_ret)

    def set_terms(which, t, term):
        own[which, t] = term[:, :TOK]
        for r in range(ROUNDS):
            ret_stage[:, which, t, r] = term[:, TOK * (r + 1) : TOK * (r + 2)].astype(BF).reshape(8, 16, TOK)

    def share_globals(which, term):
        gg_stage[which] = term.T.reshape(2, 8, 32, HD)
        gg_half[which] = gg_stage[which, 1 - my_core].astype(BF)
        put(
            gg_half.at[which], gg_pair.at[which], send_gg.at[0], sem_gg.at[0, which], plane(my_p + 1 - 2 * my_core)
        )

    def give_globals(which):
        wait(gg_pair.at[which], sem_gg.at[0, which])
        gg_sum[which] = (gg_stage[which, my_core] + gg_pair[which].astype(F32)).astype(BF)
        keep(gg_sum.at[which, my_chip], gg.at[which, my_chip], sem_gg.at[1, which])

        each_chip(
            lambda chip: put(
                gg_sum.at[which, chip], gg.at[which, my_chip], send_gg.at[1], sem_gg.at[1, which],
                plane(chip * 2 + my_core),
            )
        )

    wait(qg.at[1], sem_qg.at[1])

    @pl.loop(0, NY)
    def _(t):
        rows = pl.ds(pl.multiple_of(t * TOK, TOK), TOK)
        gt = qg[1, t].T
        g_t[:, rows] = gt
        set_terms(1, t, mm(gt, low[rows, :512]))
        send_back(1, t)

    share_globals(1, mm(g_t[...], low[:, 512:]))

    @pl.loop(0, NY)
    def _(n):
        t = turn(n)
        wait(part.at[:, 1, n], sem_part.at[1, n])
        rows = pl.ds(pl.multiple_of(t * TOK, TOK), TOK)
        q, g = qg[0, t], qg[1, t]
        v_loc[0:TOK] = kv[1, t]
        for r in range(ROUNDS):
            v_loc[TOK * (r + 1) : TOK * (r + 2)] = part[:, 1, n, r].reshape(TOK, HD)
        gp_loc, gp_glob = mm_t(g, v_loc[...]), mm_t(g, v_glob[...])
        low_loc, low_glob = low[rows, :512], low[rows, 512:]
        centre = jnp.sum(low_loc.astype(F32) * gp_loc, axis=1, keepdims=True) + jnp.sum(
            low_glob.astype(F32) * gp_glob, axis=1, keepdims=True
        )
        sg_loc = (probs[rows, :512] * (gp_loc - centre)).astype(BF)
        sg_glob = (probs[rows, 512:] * (gp_glob - centre)).astype(BF)
        sgrad[rows] = sg_glob
        qt = q.T
        q_t[:, rows] = qt
        set_terms(0, t, mm(qt, sg_loc) * SCALE)

        @pl.when(n < EARLY)
        def _():
            send_back(0, t)

        od_stage[0, t] = (mm(low_loc, v_loc[...]) + mm(low_glob, v_glob[...])).astype(BF)
        od_stage[1, t] = ((mm(sg_loc, k_loc[t]) + mm(sg_glob, k_glob[...])) * SCALE).astype(BF)

        @pl.when(n == NY - 1)
        def _():
            keep(od_stage.at[0, t], cols(o_out, my_y), sem_out.at[0])
            keep(od_stage.at[1, t], cols(dq_out, my_y), sem_out.at[1])

        @pl.when(n < NY - 1)
        def _():
            put(od_stage.at[0, t], cols(o_out, my_y), send_od, sem_out.at[0], line(t))
            put(od_stage.at[1, t], cols(dq_out, my_y), send_od, sem_out.at[1], line(t))

    def add_and_send():
        wait(ret, sem_ret)

        @pl.loop(0, NY)
        def _(n):
            t = far(n)
            dst, sem = tot.at[my_p // 2, my_core, t], sem_tot.at[my_core, t]

            named = [[matches[r, shard(p, t)] for r in range(ROUNDS)] for p in range(NP)]
            for p in range(NP):
                terms = [ret[named[p][r], r].astype(F32) for r in range(ROUNDS)]
                tot_stage[p, t] = (terms[0] + terms[1] + terms[2]).astype(BF)

            each_other(lambda p: put(tot_stage.at[p, t], dst, send_tot, sem, plane(p)))
            keep(tot_stage.at[my_p, t], dst, sem)

    def finish(which, out):
        wait(gg.at[which], sem_gg.at[1, which])
        gsum[...] = jnp.sum(gg[which].astype(F32), axis=0).astype(BF)

        @pl.loop(0, NY)
        def _(n):
            t = far(n)
            wait(tot.at[:, which, t], sem_tot.at[which, t])
            rows = gsum[pl.ds(pl.multiple_of((t // 4) * 16, 16), 16)]
            back = own[which, t] + tot[:, which, t].reshape(HD, TOK).astype(F32)
            there = lax.dot_general(aux_all[t, :16], rows, (((0,), (0,)), ((), ())), preferred_element_type=F32)
            kvg_stage[which, t] = (back.T + there).astype(BF)

            @pl.when(n == NY - 1)
            def _():
                keep(kvg_stage.at[which, t], cols(out, my_y), sem_out.at[2 + which])

            @pl.when(n < NY - 1)
            def _():
                put(kvg_stage.at[which, t], cols(out, my_y), send_kvg, sem_out.at[2 + which], line(t))

    give_globals(1)

    @pl.when(my_core == 1)
    def _():
        add_and_send()

    @pl.loop(EARLY, NY)
    def _(n):
        send_back(0, turn(n))

    share_globals(0, mm(q_t[...], sgrad[...]) * SCALE)
    finish(1, dv_out)
    give_globals(0)

    @pl.when(my_core == 0)
    def _():
        add_and_send()

    finish(0, dk_out)

    for n, out in enumerate((o_out, dq_out, dk_out, dv_out)):
        wait(out, sem_out.at[n])
    wait(aux_all.at[: NY - 1], send_aux)
    for sem in (send_kv, send_qg, send_od, send_kvg):
        wait(kv.at[:, : NY - 1], sem)
    for sem in (send_inter, send_tot):
        wait(tot_stage.at[: NP - 1], sem)
    for sem in (send_part, send_ret):
        wait(stage.at[: NP - 1], sem)
    wait(gl_all.at[0, :7], send_gl.at[0])
    wait(gl_all.at[0], send_gl.at[1])
    wait(gg_half, send_gg.at[0])
    wait(gg.at[:, :7], send_gg.at[1])


def hand_out(*refs):
    ins, outs, held, sems = refs[:4], refs[4:8], refs[8], refs[9]
    come = [pltpu.make_async_copy(a, held.at[n], sems.at[0, n]) for n, a in enumerate(ins)]
    go = [pltpu.make_async_copy(held.at[n], b, sems.at[1, n]) for n, b in enumerate(outs)]
    for copy in come:
        copy.start()
    for n in range(4):
        come[n].wait()
        go[n].start()
    for copy in go:
        copy.wait()


def local(queries, key_rows, value_rows, cotangent, matches, active, global_pos):
    out = jax.ShapeDtypeStruct(queries.shape, BF)
    smem, hbm = (pl.BlockSpec(memory_space=m) for m in (pltpu.SMEM, pltpu.HBM))
    dma = pltpu.SemaphoreType.DMA
    shapes = [
        ((4, NY, TOK, HD), BF),
        ((32, TOK), BF),
        ((NY, 32, TOK), BF),
        ((2, NY, TOK, HD), BF),
        ((2, NY, TOK, HD), BF),
        ((NP * NY, 16, HD), BF),
        ((NP, NY, ROUNDS, 16, HD), BF),
        ((8, 2, NY, ROUNDS, 16, HD), BF),
        ((2, 32, HD), BF),
        ((2, 8, 2, 32, HD), BF),
        ((NY, 512, HD), BF),
        ((512, HD), BF),
        ((512, HD), BF),
        ((512, HD), BF),
        ((NY * TOK, 1024), F32),
        ((NY * TOK, 1024), BF),
        ((NY * TOK, 512), BF),
        ((HD, NY * TOK), BF),
        ((HD, NY * TOK), BF),
        ((8, 2, NY, ROUNDS, 16, TOK), BF),
        ((NP * NY, ROUNDS, 16, TOK), BF),
        ((NP, NY, 16, TOK), BF),
        ((8, 2, NY, 16, TOK), BF),
        ((2, NY, HD, TOK), F32),
        ((2, 2, 8, 32, HD), F32),
        ((2, 8, 32, HD), BF),
        ((2, 8, 32, HD), BF),
        ((2, 8, 32, HD), BF),
        ((2, 8, 32, HD), BF),
        ((32, HD), BF),
        ((2, NY, TOK, HD), BF),
        ((2, NY, TOK, HD), BF),
    ]
    results = pl.pallas_call(
        kernel,
        out_shape=(out,) * 4,
        in_specs=[smem] * 3 + [hbm] * 4,
        out_specs=(hbm,) * 4,
        scratch_shapes=[pltpu.VMEM(*s) for s in shapes]
        + [dma((4,)), dma, dma((2, NY)), dma((2,)), dma, dma((2, NY)), dma((2,)), dma, dma((2, NY)), dma((2, 2)), dma((4,))]
        + [dma] * 5
        + [dma((2,)), dma, dma, dma((2,)), dma, dma],
        compiler_params=pltpu.CompilerParams(
            collective_id=0, has_side_effects=True, vmem_limit_bytes=63 * 1024 * 1024
        ),
        cost_estimate=pl.CostEstimate(flops=1_700_000_000, bytes_accessed=2_000_000, transcendentals=1_048_576),
    )(matches, active.reshape(ROUNDS), global_pos, queries, key_rows, value_rows, cotangent)
    return pl.pallas_call(
        hand_out,
        out_shape=(out,) * 4,
        in_specs=[hbm] * 4,
        out_specs=(hbm,) * 4,
        scratch_shapes=[pltpu.VMEM((4, TOK, NY * HD), BF), dma((2, 4))],
        compiler_params=pltpu.CompilerParams(vmem_limit_bytes=63 * 1024 * 1024),
    )(*results)


def solution(mesh):
    rows = P(("batch", "seq"), None)
    return jax.shard_map(
        local,
        mesh=mesh,
        in_specs=(rows, rows, rows, rows, P("batch", None), P("batch", "seq"), P(("batch", "seq"))),
        out_specs=(rows,) * 4,
        check_vma=False,
    )
```
